512 devices in a mesh: feat: 16 (over x, y), label: 32 (over z, core).
Axes of the slice: x: 4, y: 4, z: 16, core: 2. Of those that a mesh axis runs over, the one named last changes fastest.
Arguments:
- doc_blocks: int32 [384, 8], replicated, may hold values from 0 to 511, all different within a row
- doc_counts: int32 [384], replicated, may hold values from 1 to 8
- doc_values: bfloat16 [384, 8, 256], replicated, may hold values from 0.049804688 to 2
- pos_labels: int32 [384, 8], replicated, may hold values from 0 to 131071, as said below
- neg_labels: int32 [384, 24], replicated, may hold values from 0 to 131071, as said below
- in_weight: bfloat16 [512, 256, 2048], P('feat', None, 'label'), may hold values from -0.1875 to 0.1875
- out_weight: bfloat16 [131072, 2048], P(('feat', 'label')), may hold values from -0.29882812 to 0.29882812
Outputs:
- in_grad: bfloat16 [512, 256, 2048], P('feat', None, 'label')
- out_grad: bfloat16 [131072, 2048], P(('feat', 'label'))
The draws below stay inside these ranges and needn't reach their ends.
Inputs may be any that keep to these rules, and one draw needn't show every extreme that they name: The ids in one row of doc_blocks are distinct. `pos_labels`: label c is held by the device of linear index c // 256 (feat index times the size of label plus label index); taken together with neg_labels, every device's labels are named by exactly 24 of the listed pairs. `neg_labels`: see pos_labels.
All inputs are finite; a program needn't handle non-finite values.
Results may differ from the reference program's by a relative error of at most 0.0065.
Values may be sent and summed in bfloat16 or wider, within the bound.
No kernel may reach another device: no remote copies, remote signals or barrier semaphores. Data moves between devices by JAX's collectives and lax.ppermute only.
A program may use at most 128 MiB of HBM per device.

```python
import math
import jax
import jax.numpy as jnp
from jax import lax

H = 2048
BLOCK = 256
LAB_DEV = 256
DOCS = 384
BPD = 8
POS = 8
NEG = 24
NB = 512
LABELS = 131072
PAIR_DEV = 24


def label_pairs(key):
    inner = jax.random.fold_in(key, 7)
    first_key, second_key = jax.random.split(inner)
    owners = jnp.tile(jnp.arange(LABELS // LAB_DEV, dtype=jnp.int32), PAIR_DEV)
    owners = jax.random.permutation(first_key, owners)
    within = jax.random.randint(second_key, (DOCS * (POS + NEG),), 0, LAB_DEV, dtype=jnp.int32)
    return (owners * LAB_DEV + within).reshape(DOCS, POS + NEG)


def draw_pos_labels(key, part):
    return label_pairs(key)[:, :POS]


def draw_neg_labels(key, part):
    return label_pairs(key)[:, POS:]


def touch_ends(values, own_key, smallest, top_value):
    shape = values.shape
    place = [jax.random.randint(jax.random.fold_in(own_key, axis), (), 0, shape[axis]) for axis in range(len(shape))]
    values = values.at[tuple(place)].set(smallest)
    longest = shape.index(max(shape))
    place[longest] = (place[longest] + 1) % shape[longest]
    return values.at[tuple(place)].set(top_value)


def levels(stream_key, dims, cuts, low, largest):
    gain = 1.0
    for position, shards_of in cuts:
        draws = jax.random.uniform(jax.random.fold_in(jax.random.fold_in(stream_key, 6), position), (shards_of,), jnp.float32, low / len(cuts), largest / len(cuts))
        gain = gain * jnp.repeat(jnp.exp(draws), dims[position] // shards_of).reshape((-1,) + (1,) * (len(dims) - 1 - position))
    return gain


def picks_of(rng, rows, number_of, top, lift):
    ranking = jax.random.permutation(jax.random.fold_in(rng, 1), number_of)
    boost = ranking
    for power in range(3):
        boost = boost * boost // number_of
    boost = boost * lift // number_of
    chance = jax.random.randint(jax.random.fold_in(rng, 2), (rows, number_of), 0, 4096) + boost
    sure = jax.random.permutation(jax.random.fold_in(rng, 3), rows)[jnp.arange(number_of) % rows]
    chance = jnp.where(jnp.arange(rows)[:, None] == sure[None, :], 1 << 14, chance)
    priority = chance * number_of + jnp.arange(number_of)
    return lax.top_k(priority.astype(jnp.int32), top)[1].astype(jnp.int32)


def noise(stream_key, dims, deviation, bound, cuts=(), kind=jnp.bfloat16):
    drawn = deviation * jax.random.normal(stream_key, dims, jnp.float32)
    if cuts:
        drawn = drawn * levels(stream_key, dims, cuts, -0.22, 0.18)
    return jnp.clip(drawn, -bound, bound).astype(kind)


def setup_inputs(seed: int = 0) -> dict:
    keys = jax.random.split(jax.random.key(seed), 8)
    doc_blocks = picks_of(keys[0], DOCS, NB, BPD, 256)
    doc_counts = touch_ends(jax.random.randint(keys[1], (DOCS,), 1, BPD + 1), jax.random.fold_in(keys[1], 1), 1, BPD).astype(jnp.int32)
    doc_values = jnp.clip(jnp.exp(jax.random.uniform(keys[2], (DOCS, BPD, BLOCK), jnp.float32, math.log(0.049804688), math.log(2.0))), 0.049804688, 2.0).astype(jnp.bfloat16)
    pos_labels = draw_pos_labels(jax.random.fold_in(keys[7], 71), 0)
    neg_labels = draw_neg_labels(jax.random.fold_in(keys[7], 71), 0)
    in_weight = noise(keys[5], (NB, BLOCK, H), (BLOCK * 4) ** -0.5, 0.1875, ((0, 16), (2, 32)))
    out_weight = noise(keys[6], (LABELS, H), 0.05, 0.29882812, ((0, 512),))
    return {"doc_blocks": doc_blocks, "doc_counts": doc_counts, "doc_values": doc_values, "pos_labels": pos_labels, "neg_labels": neg_labels, "in_weight": in_weight, "out_weight": out_weight}


def reference(doc_blocks, doc_counts, doc_values, pos_labels, neg_labels, in_weight, out_weight):
    slots = jnp.arange(BPD, dtype=jnp.int32)

    def one_doc(items):
        ids, vals, count = items
        valid = (slots < count).astype(jnp.float32)
        used = vals.astype(jnp.float32) * valid[:, None]
        rows = in_weight[ids].astype(jnp.float32)
        return jnp.einsum("kv,kvh->h", used, rows)

    pre = lax.map(one_doc, (doc_blocks, doc_values, doc_counts))
    hidden = jax.nn.silu(pre).astype(jnp.bfloat16)
    labels = jnp.concatenate([pos_labels, neg_labels], axis=1)
    target = jnp.concatenate([jnp.ones((DOCS, POS), jnp.float32), jnp.zeros((DOCS, NEG), jnp.float32)], axis=1)
    picked = out_weight[labels].astype(jnp.float32)
    hidden_f = hidden.astype(jnp.float32)
    logit = jnp.einsum("dh,dkh->dk", hidden_f, picked)
    pair_grad = (jax.nn.sigmoid(logit) - target).astype(jnp.bfloat16).astype(jnp.float32)
    same = (labels[:, :, None] == labels[:, None, :]).astype(jnp.float32)
    total = jnp.einsum("dkj,dj->dk", same, pair_grad).astype(jnp.bfloat16).astype(jnp.float32)
    width = POS + NEG
    earlier = (jnp.arange(width)[None, :] < jnp.arange(width)[:, None]).astype(jnp.float32)
    repeats = jnp.einsum("dkj,kj->dk", same, earlier)
    label_grad = jnp.where(repeats > 0.5, 0.0, total)
    out_grad = jnp.zeros((LABELS, H), jnp.float32).at[labels].add(label_grad[:, :, None] * hidden_f[:, None, :])
    hidden_grad = jnp.einsum("dk,dkh->dh", label_grad, picked)
    sig = jax.nn.sigmoid(pre)
    pre_grad = (hidden_grad * sig * (1.0 + pre * (1.0 - sig))).astype(jnp.bfloat16).astype(jnp.float32)

    def add_doc(acc, items):
        ids, vals, count, grad_row = items
        valid = (slots < count).astype(jnp.float32)
        used = vals.astype(jnp.float32) * valid[:, None]
        return acc.at[ids].add(used[:, :, None] * grad_row[None, None, :]), None

    in_grad, _ = lax.scan(add_doc, jnp.zeros((NB, BLOCK, H), jnp.float32), (doc_blocks, doc_values, doc_counts, pre_grad))
    return in_grad.astype(jnp.bfloat16), out_grad.astype(jnp.bfloat16)
```

```python
import jax
import jax.numpy as jnp
from jax import lax
from jax.sharding import PartitionSpec as P

F32 = jnp.float32
BF16 = jnp.bfloat16
ROWS = 32


def spread(part):
    shards = lax.axis_size("feat")
    copies = jnp.broadcast_to(part.astype(BF16)[None], (shards,) + part.shape)
    arrived = lax.all_to_all(copies, "feat", 0, 0, tiled=True)
    return jnp.sum(arrived.astype(F32), axis=0)


def on_device(doc_blocks, doc_counts, doc_values, pos_labels, neg_labels, in_weight, out_weight):
    block_count, block_size, col_count = in_weight.shape
    doc_total, slot_count = doc_blocks.shape
    lab_count, hidden_width = out_weight.shape
    feat_index = lax.axis_index("feat")
    label_index = lax.axis_index("label")
    owners = lax.axis_size("label")
    half = ROWS // 2

    local_ids = doc_blocks - feat_index * block_count
    slots = jnp.arange(slot_count, dtype=jnp.int32)
    valid = slots[None, :] < doc_counts[:, None]
    picks = (
        local_ids[:, :, None] == jnp.arange(block_count, dtype=jnp.int32)[None, None, :]
    ) & valid[:, :, None]
    dense = jnp.einsum(
        "dkb,dkv->dbv", picks.astype(BF16), doc_values, preferred_element_type=F32
    ).astype(BF16)
    weight_t = jnp.swapaxes(in_weight, 1, 2)
    partial_t = jnp.einsum("bhv,dbv->hd", weight_t, dense, preferred_element_type=F32)

    labels_t = jnp.concatenate([pos_labels.T, neg_labels.T], axis=0)
    rel = labels_t // lab_count - feat_index * owners
    count = jnp.sum(
        (rel[None] == jnp.arange(owners, dtype=jnp.int32)[:, None, None]).astype(F32), axis=1
    )
    docs = jnp.arange(doc_total, dtype=jnp.int32)
    before = (docs[:, None] < docs[None, :]).astype(BF16)
    base = jnp.dot(count.astype(BF16), before, preferred_element_type=F32)
    place = jnp.where(count > 0, base, -1.0)
    ranks = jnp.arange(ROWS, dtype=jnp.int32).astype(F32)
    pick_rows = (place[:, None, :] == ranks[None, :, None]).astype(BF16)
    pick_low = pick_rows[:, :half].reshape(owners * half, doc_total)
    pick_high = pick_rows[:, half:].reshape(owners * half, doc_total)

    pre_t = spread(partial_t)
    hidden_t = jax.nn.silu(pre_t).astype(BF16)
    nt = (((1,), (1,)), ((), ()))
    low = lax.dot_general(pick_low, hidden_t, nt, preferred_element_type=F32)
    high = lax.dot_general(pick_high, hidden_t, nt, preferred_element_type=F32)
    sent = jnp.concatenate([low, high], axis=1).astype(BF16).reshape(owners, half, 2 * col_count)
    got = lax.all_to_all(sent, "label", 0, 0, tiled=True)
    rows = got.reshape(owners, half, 2, col_count).transpose(2, 1, 0, 3).reshape(ROWS, hidden_width)

    logit = lax.dot_general(rows, out_weight, nt, preferred_element_type=F32)
    own = labels_t - (feat_index * owners + label_index) * lab_count
    own = jnp.where((own >= 0) & (own < lab_count), own + 1, 0).astype(BF16)
    own_place = lax.dynamic_slice_in_dim(place, label_index, 1, 0)
    own_pick = (own_place == ranks[:, None]).astype(BF16)
    row_labels = lax.dot_general(own_pick, own, nt, preferred_element_type=F32)
    names = jnp.arange(1, lab_count + 1, dtype=jnp.int32).astype(F32)
    hits = (row_labels[:, :, None] == names[None, None, :]).astype(F32)
    pos_slots = pos_labels.shape[1]
    pos_count = jnp.sum(hits[:, :pos_slots], axis=1)
    neg_count = jnp.sum(hits[:, pos_slots:], axis=1)
    sig = jax.nn.sigmoid(logit)
    grad_pos = (sig - 1.0).astype(BF16).astype(F32)
    grad_neg = sig.astype(BF16).astype(F32)
    label_grad = (pos_count * grad_pos + neg_count * grad_neg).astype(BF16)
    out_grad = lax.dot_general(
        label_grad, rows, (((0,), (0,)), ((), ())), preferred_element_type=F32
    ).astype(BF16)
    terms = jnp.dot(label_grad, out_weight, preferred_element_type=F32).astype(BF16)
    back = terms.reshape(2, half, owners, col_count).transpose(2, 1, 0, 3)
    back = back.reshape(owners, half, 2 * col_count)
    came = lax.all_to_all(back, "label", 0, 0, tiled=True).reshape(owners * half, 2 * col_count)
    tn = (((0,), (0,)), ((), ()))
    grad_part = lax.dot_general(
        came[:, :col_count], pick_low, tn, preferred_element_type=F32
    ) + lax.dot_general(came[:, col_count:], pick_high, tn, preferred_element_type=F32)

    hidden_grad = spread(grad_part)
    gate = jax.nn.sigmoid(pre_t)
    pre_grad = (hidden_grad * gate * (1.0 + pre_t * (1.0 - gate))).astype(BF16)
    in_grad = jnp.einsum("hd,dbv->bhv", pre_grad, dense, preferred_element_type=F32).astype(BF16)
    return (jnp.swapaxes(in_grad, 1, 2), out_grad)


def solution(mesh):
    placed = (P(), P(), P(), P(), P(), P("feat", None, "label"), P(("feat", "label"), None))
    return jax.shard_map(
        on_device,
        mesh=mesh,
        in_specs=placed,
        out_specs=(P("feat", None, "label"), P(("feat", "label"), None)),
        check_vma=False,
    )
```

```python
import jax
import jax.numpy as jnp
from jax import lax
from jax.experimental import pallas as pl
from jax.experimental.pallas import tpu as pltpu
from jax.sharding import PartitionSpec as P

F32 = jnp.float32
BF16 = jnp.bfloat16
ROWS = 32


GROUP = 32
CHUNK = 256
NOTES = 16
VMEM = pl.BlockSpec(memory_space=pltpu.VMEM)
SMEM = pl.BlockSpec(memory_space=pltpu.SMEM)
HBM = pl.BlockSpec(memory_space=pltpu.HBM)
NT = (((1,), (1,)), ((), ()))


def iota(shape, dim):
    return lax.broadcasted_iota(jnp.int32, shape, dim)


def one_hot(left, right):
    return jnp.where(left == right, 1.0, 0.0).astype(BF16)


def owner_rows(notes, docs):
    held = notes.astype(F32)
    doc = held[2:3] * float(GROUP) + held[1:2]
    return one_hot(iota((docs, 1), 0).astype(F32), doc), held[0:1]


def forward_kernel(
    code_hbm, values_hbm, weight_hbm, packed_hbm, count_ref, out_ref,
    code_ref, values, weight, rank_ref, stage, total_ref, sems, weight_sem, stage_sem,
):
    groups = values.shape[0]
    blocks, cols, width = weight.shape
    docs = groups * GROUP
    code_load = pltpu.make_async_copy(code_hbm, code_ref, stage_sem)
    code_load.start()
    loads = [
        pltpu.make_async_copy(values_hbm.at[g], values.at[g], sems.at[g]) for g in range(groups)
    ]
    for load in loads:
        load.start()
    weight_load = pltpu.make_async_copy(weight_hbm, weight, weight_sem)
    weight_load.start()

    code_load.wait()
    code = code_ref[...].astype(F32)
    pad_groups, lanes = code.shape
    listed = jnp.where(code >= 0.0, 1.0, 0.0)
    listed16 = listed.astype(BF16)
    ahead = jnp.where(iota((lanes, lanes), 0) < iota((lanes, lanes), 1), 1.0, 0.0).astype(BF16)
    above = jnp.where(
        iota((pad_groups, pad_groups), 0) > iota((pad_groups, pad_groups), 1), 1.0, 0.0
    ).astype(BF16)
    upper = jnp.dot(above, listed16, preferred_element_type=F32).astype(BF16)
    rank = jnp.dot(listed16, ahead, preferred_element_type=F32) + jnp.dot(
        upper, jnp.ones((lanes, lanes), BF16), preferred_element_type=F32
    )
    rank_ref[...] = jnp.where(code >= 0.0, rank, -1.0)
    count = jnp.sum(listed).astype(jnp.int32)
    chunks = jnp.maximum((count + CHUNK - 1) // CHUNK, 1)
    count_ref[0, 0] = chunks
    note_row = iota((NOTES, lanes), 0)
    lane_doc = (iota((NOTES, lanes), 1) // (lanes // GROUP)).astype(F32)

    def add_chunk(chunk, wait):
        spots = (iota((CHUNK, 1), 0) + chunk * CHUNK).astype(F32)
        rows = jnp.zeros((CHUNK, width), F32)
        notes = jnp.zeros((NOTES, CHUNK), F32)
        for g in range(groups):
            pick = one_hot(spots, rank_ref[g : g + 1])
            told = jnp.where(note_row == 0, code_ref[g : g + 1].astype(F32), 0.0)
            told = jnp.where(note_row == 1, lane_doc, told)
            told = jnp.where(note_row == 2, float(g), told).astype(BF16)
            notes += lax.dot_general(told, pick, NT, preferred_element_type=F32)
            if wait:
                loads[g].wait()
            rows += jnp.dot(pick, values[g], preferred_element_type=F32)
        stage[:CHUNK] = rows.astype(BF16)
        stage[CHUNK:] = notes.astype(BF16)
        save = pltpu.make_async_copy(stage, packed_hbm.at[chunk], stage_sem)
        save.start()
        doc_rows, block = owner_rows(stage[CHUNK:], docs)
        if wait:
            weight_load.wait()
        every = lax.dot_general(
            weight[...].reshape(blocks * cols, width), stage[:CHUNK], NT, preferred_element_type=F32
        )
        part = jnp.zeros((cols, CHUNK), F32)
        for b in range(blocks):
            part += jnp.where(block == float(b), every[b * cols : (b + 1) * cols], 0.0)
        high = part.astype(BF16)
        low = (part - high.astype(F32)).astype(BF16)
        both = lax.dot_general(
            jnp.concatenate([high, low], axis=0), doc_rows, NT, preferred_element_type=F32
        )
        save.wait()
        return both[:cols] + both[cols:]

    total_ref[...] = add_chunk(0, True)

    @pl.when(chunks > 1)
    def _():
        @pl.loop(1, chunks)
        def _(chunk):
            total_ref[...] += add_chunk(chunk, False)

    part = total_ref[...].astype(BF16)
    for shard in range(out_ref.shape[0]):
        out_ref[shard] = part


def forward(code, values, weight_t, shards):
    blocks, cols, width = weight_t.shape
    groups, lanes, _ = values.shape
    docs = groups * GROUP
    most = -(-groups * lanes // CHUNK)
    return pl.pallas_call(
        forward_kernel,
        out_shape=(
            jax.ShapeDtypeStruct((most, CHUNK + NOTES, width), BF16),
            jax.ShapeDtypeStruct((1, 1), jnp.int32),
            jax.ShapeDtypeStruct((shards, cols, docs), BF16),
        ),
        in_specs=[HBM, HBM, HBM],
        out_specs=(HBM, SMEM, VMEM),
        scratch_shapes=[
            pltpu.VMEM(code.shape, jnp.int32),
            pltpu.VMEM(values.shape, BF16),
            pltpu.VMEM(weight_t.shape, BF16),
            pltpu.VMEM(code.shape, F32),
            pltpu.VMEM((CHUNK + NOTES, width), BF16),
            pltpu.VMEM((cols, docs), F32),
            pltpu.SemaphoreType.DMA((groups,)),
            pltpu.SemaphoreType.DMA(()),
            pltpu.SemaphoreType.DMA(()),
        ],
        compiler_params=pltpu.CompilerParams(vmem_limit_bytes=60 << 20),
    )(code, values, weight_t)


def backward_kernel(count_ref, parts_ref, pre_ref, packed_hbm, out_ref, stage, grad_ref, total_ref, sem):
    blocks, cols, width = out_ref.shape
    docs = pre_ref.shape[1]
    chunks = count_ref[0, 0]
    first = pltpu.make_async_copy(packed_hbm.at[0], stage, sem)
    first.start()
    hidden_grad = parts_ref[0].astype(F32)
    for shard in range(1, parts_ref.shape[0]):
        hidden_grad += parts_ref[shard].astype(F32)
    pre = pre_ref[...]
    gate = jax.nn.sigmoid(pre)
    grad_ref[...] = (hidden_grad * gate * (1.0 + pre * (1.0 - gate))).astype(BF16)
    first.wait()

    def product():
        doc_rows, block = owner_rows(stage[CHUNK:], docs)
        grads = jnp.dot(grad_ref[...], doc_rows, preferred_element_type=F32)
        grads = [jnp.where(block == float(b), grads, 0.0).astype(BF16) for b in range(blocks)]
        return jnp.dot(
            jnp.concatenate(grads, axis=0), stage[:CHUNK], preferred_element_type=F32
        ).reshape(blocks, cols, width)

    @pl.when(chunks <= 1)
    def _():
        out_ref[...] = product().astype(BF16)

    @pl.when(chunks > 1)
    def _():
        total_ref[...] = product()

        @pl.loop(1, chunks)
        def _(chunk):
            later = pltpu.make_async_copy(packed_hbm.at[chunk], stage, sem)
            later.start()
            later.wait()
            total_ref[...] += product()

        out_ref[...] = total_ref[...].astype(BF16)


def backward(count, parts, pre_t, packed, blocks):
    cols, docs = pre_t.shape
    width = packed.shape[2]
    return pl.pallas_call(
        backward_kernel,
        out_shape=jax.ShapeDtypeStruct((blocks, cols, width), BF16),
        in_specs=[SMEM, VMEM, VMEM, HBM],
        out_specs=VMEM,
        scratch_shapes=[
            pltpu.VMEM(packed.shape[1:], BF16),
            pltpu.VMEM((cols, docs), BF16),
            pltpu.VMEM((blocks, cols, width), F32),
            pltpu.SemaphoreType.DMA(()),
        ],
        compiler_params=pltpu.CompilerParams(vmem_limit_bytes=16 << 20),
    )(count, parts, pre_t, packed)


def row_picks(place_ref):
    owners = place_ref.shape[0]
    half = ROWS // 2
    low_rank = iota((half, 1), 0).astype(F32)
    places = [place_ref[o : o + 1] for o in range(owners)]
    low = jnp.concatenate([jnp.where(low_rank == p, 1.0, 0.0) for p in places], axis=0)
    high = jnp.concatenate([jnp.where(low_rank + half == p, 1.0, 0.0) for p in places], axis=0)
    return low.astype(BF16), high.astype(BF16)


def hidden_kernel(parts_ref, place_ref, pre_ref, sent_ref):
    pre = parts_ref[0].astype(F32)
    for shard in range(1, parts_ref.shape[0]):
        pre += parts_ref[shard].astype(F32)
    pre_ref[...] = pre
    hidden = jax.nn.silu(pre).astype(BF16)
    none = jnp.zeros_like(hidden)
    low, high = row_picks(place_ref)
    rows = lax.dot_general(
        low, jnp.concatenate([hidden, none], axis=0), NT, preferred_element_type=F32
    ) + lax.dot_general(
        high, jnp.concatenate([none, hidden], axis=0), NT, preferred_element_type=F32
    )
    sent_ref[...] = rows.astype(BF16).reshape(sent_ref.shape)


def label_kernel(got_ref, weight_ref, pos_ref, neg_ref, back_ref, rows_ref, grad_ref):
    owners, half, lanes = got_ref.shape
    cols = lanes // 2
    first = iota((half, lanes), 1) < cols
    lows, highs = [], []
    for pair in range(owners // 2):
        left = got_ref[2 * pair].astype(F32)
        right = got_ref[2 * pair + 1].astype(F32)
        lows.append(jnp.where(first, left, pltpu.roll(right, cols, 1)))
        highs.append(jnp.where(first, pltpu.roll(left, cols, 1), right))
    rows = jnp.concatenate(
        [jnp.concatenate(lows, axis=1), jnp.concatenate(highs, axis=1)], axis=0
    ).astype(BF16)
    rows_ref[...] = rows
    weight = weight_ref[...]
    logit = lax.dot_general(rows, weight, NT, preferred_element_type=F32)
    sig = jax.nn.sigmoid(logit)
    grad_pos = (sig - 1.0).astype(BF16).astype(F32)
    grad_neg = sig.astype(BF16).astype(F32)
    grad = (pos_ref[...] * grad_pos + neg_ref[...] * grad_neg).astype(BF16)
    grad_ref[...] = grad
    terms = jnp.dot(grad, weight, preferred_element_type=F32)
    for pair in range(owners // 2):
        low = terms[:half, pair * lanes : (pair + 1) * lanes]
        high = terms[half:, pair * lanes : (pair + 1) * lanes]
        back_ref[2 * pair] = jnp.where(first, low, pltpu.roll(high, cols, 1)).astype(BF16)
        back_ref[2 * pair + 1] = jnp.where(first, pltpu.roll(low, cols, 1), high).astype(BF16)


def collect_kernel(came_ref, place_ref, out_ref):
    owners, half, lanes = came_ref.shape
    cols = lanes // 2
    came = came_ref[...].reshape(owners * half, lanes)
    low, high = row_picks(place_ref)
    tn = (((0,), (0,)), ((), ()))
    part = (
        lax.dot_general(came, low, tn, preferred_element_type=F32)[:cols]
        + lax.dot_general(came, high, tn, preferred_element_type=F32)[cols:]
    ).astype(BF16)
    for shard in range(out_ref.shape[0]):
        out_ref[shard] = part


def local_call(kernel, inputs, *shapes):
    return pl.pallas_call(
        kernel,
        out_shape=tuple(jax.ShapeDtypeStruct(shape, kind) for shape, kind in shapes),
        in_specs=[VMEM] * len(inputs),
        out_specs=(VMEM,) * len(shapes),
        compiler_params=pltpu.CompilerParams(vmem_limit_bytes=16 << 20),
    )(*inputs)


def on_device(doc_blocks, doc_counts, doc_values, pos_labels, neg_labels, in_weight, out_weight):
    block_count, block_size, col_count = in_weight.shape
    doc_total, slot_count = doc_blocks.shape
    lab_count, hidden_width = out_weight.shape
    feat_index = lax.axis_index("feat")
    label_index = lax.axis_index("label")
    owners = lax.axis_size("label")
    shards = lax.axis_size("feat")
    half = ROWS // 2

    local_ids = doc_blocks - feat_index * block_count
    slots = jnp.arange(slot_count, dtype=jnp.int32)
    listed = (slots[None, :] < doc_counts[:, None]) & (local_ids >= 0) & (local_ids < block_count)
    groups = doc_total // GROUP
    code = jnp.where(listed, local_ids, -1).reshape(groups, GROUP * slot_count)
    code = jnp.pad(code, ((0, -groups % 8), (0, 0)), constant_values=-1)
    packed, chunks, copies = forward(
        code,
        doc_values.reshape(groups, GROUP * slot_count, block_size),
        jnp.swapaxes(in_weight, 1, 2),
        shards,
    )

    labels_t = jnp.concatenate([pos_labels.T, neg_labels.T], axis=0)
    rel = labels_t // lab_count - feat_index * owners
    count = jnp.sum(
        (rel[None] == jnp.arange(owners, dtype=jnp.int32)[:, None, None]).astype(F32), axis=1
    )
    docs = jnp.arange(doc_total, dtype=jnp.int32)
    before = (docs[:, None] < docs[None, :]).astype(BF16)
    base = jnp.dot(count.astype(BF16), before, preferred_element_type=F32)
    place = jnp.where(count > 0, base, -1.0)
    ranks = jnp.arange(ROWS, dtype=jnp.int32).astype(F32)
    nt = NT
    arrived = lax.all_to_all(copies, "feat", 0, 0, tiled=True)
    row_shape = (owners, half, 2 * col_count)
    pre_t, sent = local_call(
        hidden_kernel, (arrived, place), (copies.shape[1:], F32), (row_shape, BF16)
    )
    got = lax.all_to_all(sent, "label", 0, 0, tiled=True)

    own = labels_t - (feat_index * owners + label_index) * lab_count
    own = jnp.where((own >= 0) & (own < lab_count), own + 1, 0).astype(BF16)
    own_place = lax.dynamic_slice_in_dim(place, label_index, 1, 0)
    own_pick = (own_place == ranks[:, None]).astype(BF16)
    row_labels = lax.dot_general(own_pick, own, nt, preferred_element_type=F32)
    names = jnp.arange(1, lab_count + 1, dtype=jnp.int32).astype(F32)
    hits = (row_labels[:, :, None] == names[None, None, :]).astype(F32)
    pos_slots = pos_labels.shape[1]
    pos_count = jnp.sum(hits[:, :pos_slots], axis=1)
    neg_count = jnp.sum(hits[:, pos_slots:], axis=1)
    back, rows, label_grad = local_call(
        label_kernel,
        (got, out_weight, pos_count, neg_count),
        (row_shape, BF16),
        ((ROWS, hidden_width), BF16),
        ((ROWS, lab_count), BF16),
    )
    came = lax.all_to_all(back, "label", 0, 0, tiled=True)
    (copies,) = local_call(collect_kernel, (came, place), (copies.shape, BF16))
    parts = lax.all_to_all(copies, "feat", 0, 0, tiled=True)
    out_grad = lax.dot_general(
        label_grad, rows, (((0,), (0,)), ((), ())), preferred_element_type=F32
    ).astype(BF16)
    in_grad = backward(chunks, parts, pre_t, packed, block_count)
    return (jnp.swapaxes(in_grad, 1, 2), out_grad)


def solution(mesh):
    placed = (P(), P(), P(), P(), P(), P("feat", None, "label"), P(("feat", "label"), None))
    return jax.shard_map(
        on_device,
        mesh=mesh,
        in_specs=placed,
        out_specs=(P("feat", None, "label"), P(("feat", "label"), None)),
        check_vma=False,
    )
```

```python
import jax
import jax.numpy as jnp
from jax import lax
from jax.experimental import pallas as pl
from jax.experimental.pallas import tpu as pltpu
from jax.sharding import PartitionSpec as P

F32 = jnp.float32
BF16 = jnp.bfloat16
PAIRS = 24
QUARTER = 4


GROUP = 32
CHUNK = 256
NOTES = 16
PIECES = 4
VMEM = pl.BlockSpec(memory_space=pltpu.VMEM)
SMEM = pl.BlockSpec(memory_space=pltpu.SMEM)
HBM = pl.BlockSpec(memory_space=pltpu.HBM)
NT = (((1,), (1,)), ((), ()))


def iota(shape, dim):
    return lax.broadcasted_iota(jnp.int32, shape, dim)


def one_hot(left, right):
    return jnp.where(left == right, 1.0, 0.0).astype(BF16)


def owner_rows(notes, docs):
    held = notes.astype(F32)
    doc = held[2:3] * float(GROUP) + held[1:2]
    return one_hot(iota((docs, 1), 0).astype(F32), doc), held[0:1]


def forward_kernel(
    ids_hbm, used_hbm, values_hbm, weight_hbm, packed_hbm, count_ref, out_ref,
    ids_ref, used_ref, code_ref, values, weight, rank_ref, stage, total_ref,
    sems, weight_sem, stage_sem, id_sems,
):
    groups = values.shape[0]
    blocks, cols, width = weight.shape
    docs = groups * GROUP
    id_loads = [
        pltpu.make_async_copy(ids_hbm, ids_ref, id_sems.at[0]),
        pltpu.make_async_copy(used_hbm, used_ref, id_sems.at[1]),
    ]
    for load in id_loads:
        load.start()
    loads = [
        pltpu.make_async_copy(values_hbm.at[g], values.at[g], sems.at[g]) for g in range(groups)
    ]
    for load in loads:
        load.start()
    weight_load = pltpu.make_async_copy(weight_hbm, weight, weight_sem)
    weight_load.start()

    for load in id_loads:
        load.wait()
    slots, _ = ids_ref.shape
    lanes = GROUP * slots
    local = ids_ref[...] - lax.axis_index("feat") * blocks
    inside = (local >= 0) & (local < blocks) & (iota((slots, 1), 0) < used_ref[...])
    ids = jnp.where(inside, local, -1).astype(F32)
    ids = jnp.concatenate([ids[:, g * GROUP : (g + 1) * GROUP] for g in range(groups)], axis=0)
    spread = one_hot(iota((GROUP, lanes), 0), iota((GROUP, lanes), 1) // slots)
    wide = jnp.dot(ids.astype(BF16), spread, preferred_element_type=F32)
    own_slot = iota(wide.shape, 0) % slots == iota(wide.shape, 1) % slots
    wide = jnp.where(own_slot, wide, 0.0).reshape(groups, slots, lanes)
    pad_groups = code_ref.shape[0]
    code_ref[...] = jnp.full(code_ref.shape, -1.0, F32)
    code_ref[:groups] = jnp.sum(wide, axis=1)
    code = code_ref[...]
    listed = jnp.where(code >= 0.0, 1.0, 0.0)
    listed16 = listed.astype(BF16)
    ahead = jnp.where(iota((lanes, lanes), 0) < iota((lanes, lanes), 1), 1.0, 0.0).astype(BF16)
    above = jnp.where(
        iota((pad_groups, pad_groups), 0) > iota((pad_groups, pad_groups), 1), 1.0, 0.0
    ).astype(BF16)
    upper = jnp.dot(above, listed16, preferred_element_type=F32).astype(BF16)
    rank = jnp.dot(listed16, ahead, preferred_element_type=F32) + jnp.dot(
        upper, jnp.ones((lanes, lanes), BF16), preferred_element_type=F32
    )
    rank_ref[...] = jnp.where(code >= 0.0, rank, -1.0)
    count = jnp.sum(listed).astype(jnp.int32)
    chunks = jnp.maximum((count + CHUNK - 1) // CHUNK, 1)
    count_ref[0, 0] = chunks
    note_row = iota((NOTES, lanes), 0)
    lane_doc = (iota((NOTES, lanes), 1) // (lanes // GROUP)).astype(F32)

    def add_chunk(chunk, wait):
        spots = (iota((CHUNK, 1), 0) + chunk * CHUNK).astype(F32)
        rows = jnp.zeros((CHUNK, width), F32)
        notes = jnp.zeros((NOTES, CHUNK), F32)
        for g in range(groups):
            pick = one_hot(spots, rank_ref[g : g + 1])
            told = jnp.where(note_row == 0, code_ref[g : g + 1], 0.0)
            told = jnp.where(note_row == 1, lane_doc, told)
            told = jnp.where(note_row == 2, float(g), told).astype(BF16)
            notes += lax.dot_general(told, pick, NT, preferred_element_type=F32)
            if wait:
                loads[g].wait()
            rows += jnp.dot(pick, values[g], preferred_element_type=F32)
        stage[:CHUNK] = rows.astype(BF16)
        stage[CHUNK:] = notes.astype(BF16)
        save = pltpu.make_async_copy(stage, packed_hbm.at[chunk], stage_sem)
        save.start()
        doc_rows, block = owner_rows(stage[CHUNK:], docs)
        if wait:
            weight_load.wait()
        every = lax.dot_general(
            weight[...].reshape(blocks * cols, width), stage[:CHUNK], NT, preferred_element_type=F32
        )
        part = jnp.zeros((cols, CHUNK), F32)
        for b in range(blocks):
            part += jnp.where(block == float(b), every[b * cols : (b + 1) * cols], 0.0)
        high = part.astype(BF16)
        low = (part - high.astype(F32)).astype(BF16)
        both = lax.dot_general(
            jnp.concatenate([high, low], axis=0), doc_rows, NT, preferred_element_type=F32
        )
        save.wait()
        return both[:cols] + both[cols:]

    total_ref[...] = add_chunk(0, True)

    @pl.when(chunks > 1)
    def _():
        @pl.loop(1, chunks)
        def _(chunk):
            total_ref[...] += add_chunk(chunk, False)

    part = total_ref[...].astype(BF16)
    for shard in range(out_ref.shape[0]):
        out_ref[shard] = part


def forward(ids, used, values, weight_t, shards):
    blocks, cols, width = weight_t.shape
    groups, lanes, _ = values.shape
    docs = groups * GROUP
    most = -(-groups * lanes // CHUNK)
    code_shape = (-(-groups // 8) * 8, lanes)
    return pl.pallas_call(
        forward_kernel,
        out_shape=(
            jax.ShapeDtypeStruct((most, CHUNK + NOTES, width), BF16),
            jax.ShapeDtypeStruct((1, 1), jnp.int32),
            jax.ShapeDtypeStruct((shards, cols, docs), BF16),
        ),
        in_specs=[HBM] * 4,
        out_specs=(HBM, SMEM, VMEM),
        scratch_shapes=[
            pltpu.VMEM(ids.shape, jnp.int32),
            pltpu.VMEM(used.shape, jnp.int32),
            pltpu.VMEM(code_shape, F32),
            pltpu.VMEM(values.shape, BF16),
            pltpu.VMEM(weight_t.shape, BF16),
            pltpu.VMEM(code_shape, F32),
            pltpu.VMEM((CHUNK + NOTES, width), BF16),
            pltpu.VMEM((cols, docs), F32),
            pltpu.SemaphoreType.DMA((groups,)),
            pltpu.SemaphoreType.DMA(()),
            pltpu.SemaphoreType.DMA(()),
            pltpu.SemaphoreType.DMA((2,)),
        ],
        compiler_params=pltpu.CompilerParams(vmem_limit_bytes=60 << 20),
    )(ids, used, values, weight_t)


def backward_kernel(
    count_ref, parts_ref, pre_ref, packed_hbm, out_hbm, stage, grad_ref, total_ref, held, sem, sems
):
    blocks, cols, width = held.shape
    docs = pre_ref.shape[1]
    chunks = count_ref[0, 0]
    first = pltpu.make_async_copy(packed_hbm.at[0], stage, sem)
    first.start()
    hidden_grad = parts_ref[0].astype(F32)
    for shard in range(1, parts_ref.shape[0]):
        hidden_grad += parts_ref[shard].astype(F32)
    pre = pre_ref[...]
    gate = jax.nn.sigmoid(pre)
    grad_ref[...] = (hidden_grad * gate * (1.0 + pre * (1.0 - gate))).astype(BF16)
    first.wait()
    step = blocks // PIECES

    def slot_grads():
        doc_rows, block = owner_rows(stage[CHUNK:], docs)
        return jnp.dot(grad_ref[...], doc_rows, preferred_element_type=F32), block

    def product(grads, block, piece):
        own = [
            jnp.where(block == float(b), grads, 0.0).astype(BF16)
            for b in range(piece * step, (piece + 1) * step)
        ]
        return jnp.dot(
            jnp.concatenate(own, axis=0), stage[:CHUNK], preferred_element_type=F32
        ).reshape(step, cols, width)

    def finish(piece_of):
        saves = []
        for piece in range(PIECES):
            part = pl.ds(piece * step, step)
            held[part] = piece_of(piece).astype(BF16)
            saves.append(pltpu.make_async_copy(held.at[part], out_hbm.at[part], sems.at[piece]))
            saves[-1].start()
        for save in saves:
            save.wait()

    @pl.when(chunks <= 1)
    def _():
        grads, block = slot_grads()
        finish(lambda piece: product(grads, block, piece))

    @pl.when(chunks > 1)
    def _():
        total_ref[...] = jnp.zeros_like(total_ref)

        @pl.loop(0, chunks)
        def _(chunk):
            later = pltpu.make_async_copy(packed_hbm.at[chunk], stage, sem)
            later.start()
            later.wait()
            grads, block = slot_grads()
            for piece in range(PIECES):
                total_ref[pl.ds(piece * step, step)] += product(grads, block, piece)

        finish(lambda piece: total_ref[pl.ds(piece * step, step)])


def backward(count, parts, pre_t, packed, blocks):
    cols, docs = pre_t.shape
    width = packed.shape[2]
    return pl.pallas_call(
        backward_kernel,
        out_shape=jax.ShapeDtypeStruct((blocks, cols, width), BF16),
        in_specs=[SMEM, VMEM, VMEM, HBM],
        out_specs=HBM,
        scratch_shapes=[
            pltpu.VMEM(packed.shape[1:], BF16),
            pltpu.VMEM((cols, docs), BF16),
            pltpu.VMEM((blocks, cols, width), F32),
            pltpu.VMEM((blocks, cols, width), BF16),
            pltpu.SemaphoreType.DMA(()),
            pltpu.SemaphoreType.DMA((PIECES,)),
        ],
        compiler_params=pltpu.CompilerParams(vmem_limit_bytes=16 << 20),
    )(count, parts, pre_t, packed)


def row_picks(place_ref):
    owners, docs = place_ref.shape
    tile = 2 * QUARTER
    within = iota((tile, 1), 0)
    first = within < QUARTER
    rank = (within % QUARTER).astype(F32)
    places = [
        jnp.where(first, place_ref[o : o + 1], place_ref[o + 1 : o + 2]) for o in range(0, owners, 2)
    ]
    picks = []
    for start in (0, PAIRS // 2):
        picks.append(
            jnp.concatenate(
                [
                    jnp.where(p == rank + float(start + offset), 1.0, 0.0)
                    for offset in range(0, PAIRS // 2, QUARTER)
                    for p in places
                ],
                axis=0,
            ).astype(BF16)
        )
    return picks


def read_rows(ref):
    owners, _, lanes = ref.shape
    return [
        [
            jnp.concatenate(
                [ref[o + i, :, at : at + 128].astype(F32) for i in range(2)], axis=0
            )
            for o in range(0, owners, 2)
        ]
        for at in range(0, lanes, 128)
    ]


def write_rows(ref, group, pair, tile):
    at = group * 128
    ref[2 * pair, :, at : at + 128] = tile[:QUARTER].astype(BF16)
    ref[2 * pair + 1, :, at : at + 128] = tile[QUARTER:].astype(BF16)


def swap(tile):
    keep = (iota(tile.shape, 0) < QUARTER) == (iota(tile.shape, 1) < 64)
    return jnp.where(keep, tile, pltpu.roll(pltpu.roll(tile, QUARTER, 0), 64, 1))


def hidden_kernel(parts_ref, place_ref, pre_ref, sent_ref):
    pre = parts_ref[0].astype(F32)
    for shard in range(1, parts_ref.shape[0]):
        pre += parts_ref[shard].astype(F32)
    pre_ref[...] = pre
    hidden = jax.nn.silu(pre).astype(BF16)
    none = jnp.zeros_like(hidden)
    low, high = row_picks(place_ref)
    rows = lax.dot_general(
        low, jnp.concatenate([hidden, none], axis=0), NT, preferred_element_type=F32
    ) + lax.dot_general(
        high, jnp.concatenate([none, hidden], axis=0), NT, preferred_element_type=F32
    )
    pairs = sent_ref.shape[0] // 2
    for index in range(rows.shape[0] // 8):
        write_rows(sent_ref, index // pairs, index % pairs, rows[index * 8 : (index + 1) * 8])


def label_kernel(got_ref, weight_ref, pos_ref, neg_ref, back_ref, rows_ref, grad_ref):
    groups = [jnp.concatenate([swap(t) for t in tiles], axis=1) for tiles in read_rows(got_ref)]
    groups.append(jnp.zeros_like(groups[0]))
    rows = jnp.concatenate(groups, axis=0).astype(BF16)
    rows_ref[...] = rows
    weight = weight_ref[...]
    logit = lax.dot_general(rows, weight, NT, preferred_element_type=F32)
    sig = jax.nn.sigmoid(logit)
    grad_pos = (sig - 1.0).astype(BF16).astype(F32)
    grad_neg = sig.astype(BF16).astype(F32)
    grad = (pos_ref[...] * grad_pos + neg_ref[...] * grad_neg).astype(BF16)
    grad_ref[...] = grad
    terms = jnp.dot(grad, weight, preferred_element_type=F32)
    for group in range(PAIRS // 8):
        for pair in range(back_ref.shape[0] // 2):
            tile = terms[group * 8 : (group + 1) * 8, pair * 128 : (pair + 1) * 128]
            write_rows(back_ref, group, pair, swap(tile))


def collect_kernel(came_ref, place_ref, out_ref):
    came = jnp.concatenate([t for tiles in read_rows(came_ref) for t in tiles], axis=0).astype(BF16)
    cols = out_ref.shape[1]
    low, high = row_picks(place_ref)
    tn = (((0,), (0,)), ((), ()))
    part = (
        lax.dot_general(came, low, tn, preferred_element_type=F32)[:cols]
        + lax.dot_general(came, high, tn, preferred_element_type=F32)[cols:]
    ).astype(BF16)
    for shard in range(out_ref.shape[0]):
        out_ref[shard] = part


def local_call(kernel, inputs, *shapes):
    return pl.pallas_call(
        kernel,
        out_shape=tuple(jax.ShapeDtypeStruct(shape, kind) for shape, kind in shapes),
        in_specs=[VMEM] * len(inputs),
        out_specs=(VMEM,) * len(shapes),
        compiler_params=pltpu.CompilerParams(vmem_limit_bytes=16 << 20),
    )(*inputs)


def on_device(doc_blocks, doc_counts, doc_values, pos_labels, neg_labels, in_weight, out_weight):
    block_count, block_size, col_count = in_weight.shape
    doc_total, slot_count = doc_blocks.shape
    lab_count, hidden_width = out_weight.shape
    feat_index = lax.axis_index("feat")
    label_index = lax.axis_index("label")
    owners = lax.axis_size("label")
    shards = lax.axis_size("feat")

    groups = doc_total // GROUP
    packed, chunks, copies = forward(
        doc_blocks.T,
        doc_counts.reshape(1, doc_total),
        doc_values.reshape(groups, GROUP * slot_count, block_size),
        jnp.swapaxes(in_weight, 1, 2),
        shards,
    )

    labels_t = jnp.concatenate([pos_labels.T, neg_labels.T], axis=0)
    rel = labels_t // lab_count - feat_index * owners
    count = jnp.sum(
        (rel[None] == jnp.arange(owners, dtype=jnp.int32)[:, None, None]).astype(F32), axis=1
    )
    docs = jnp.arange(doc_total, dtype=jnp.int32)
    before = (docs[:, None] < docs[None, :]).astype(BF16)
    base = jnp.dot(count.astype(BF16), before, preferred_element_type=F32)
    place = jnp.where(count > 0, base, -1.0)
    spot = jnp.arange(PAIRS + 8, dtype=jnp.int32)
    ranks = spot // 8 * QUARTER + spot % QUARTER + spot % 8 // QUARTER * (PAIRS // 2)
    ranks = jnp.where(spot < PAIRS, ranks, -2).astype(F32)
    nt = NT
    arrived = lax.all_to_all(copies, "feat", 0, 0, tiled=True)
    row_shape = (owners, QUARTER, PAIRS * col_count // QUARTER)
    pre_t, sent = local_call(
        hidden_kernel, (arrived, place), (copies.shape[1:], F32), (row_shape, BF16)
    )
    got = lax.all_to_all(sent, "label", 0, 0, tiled=True)

    own = labels_t - (feat_index * owners + label_index) * lab_count
    own = jnp.where((own >= 0) & (own < lab_count), own + 1, 0).astype(BF16)
    own_place = lax.dynamic_slice_in_dim(place, label_index, 1, 0)
    own_pick = (own_place == ranks[:, None]).astype(BF16)
    row_labels = lax.dot_general(own_pick, own, nt, preferred_element_type=F32)
    names = jnp.arange(1, lab_count + 1, dtype=jnp.int32).astype(F32)
    hits = (row_labels[:, :, None] == names[None, None, :]).astype(F32)
    pos_slots = pos_labels.shape[1]
    pos_count = jnp.sum(hits[:, :pos_slots], axis=1)
    neg_count = jnp.sum(hits[:, pos_slots:], axis=1)
    back, rows, label_grad = local_call(
        label_kernel,
        (got, out_weight, pos_count, neg_count),
        (row_shape, BF16),
        ((PAIRS + 8, hidden_width), BF16),
        ((PAIRS + 8, lab_count), BF16),
    )
    came = lax.all_to_all(back, "label", 0, 0, tiled=True)
    (copies,) = local_call(collect_kernel, (came, place), (copies.shape, BF16))
    parts = lax.all_to_all(copies, "feat", 0, 0, tiled=True)
    out_grad = lax.dot_general(
        label_grad, rows, (((0,), (0,)), ((), ())), preferred_element_type=F32
    ).astype(BF16)
    in_grad = backward(chunks, parts, pre_t, packed, block_count)
    return (jnp.swapaxes(in_grad, 1, 2), out_grad)


def solution(mesh):
    placed = (P(), P(), P(), P(), P(), P("feat", None, "label"), P(("feat", "label"), None))
    return jax.shard_map(
        on_device,
        mesh=mesh,
        in_specs=placed,
        out_specs=(P("feat", None, "label"), P(("feat", "label"), None)),
        check_vma=False,
    )
```

```python
import functools

import jax
import jax.numpy as jnp
from jax import lax
from jax.experimental import pallas as pl
from jax.experimental.pallas import tpu as pltpu
from jax.sharding import PartitionSpec as P

F32 = jnp.float32
BF16 = jnp.bfloat16
PAIRS = 24
QUARTER = 4


GROUP = 32
CHUNK = 256
NOTES = 16
PIECES = 4
VMEM = pl.BlockSpec(memory_space=pltpu.VMEM)
SMEM = pl.BlockSpec(memory_space=pltpu.SMEM)
HBM = pl.BlockSpec(memory_space=pltpu.HBM)
NT = (((1,), (1,)), ((), ()))


def iota(shape, dim):
    return lax.broadcasted_iota(jnp.int32, shape, dim)


def one_hot(left, right):
    return jnp.where(left == right, 1.0, 0.0).astype(BF16)


def owner_rows(notes, docs):
    held = notes.astype(F32)
    doc = held[2:3] * float(GROUP) + held[1:2]
    return one_hot(iota((docs, 1), 0).astype(F32), doc), held[0:1]


def name_rows(pos_ids, neg_ids, owners, labels, base_ref, pairs_ref, pos_ref, neg_ref):
    pos_slots, docs = pos_ids.shape
    ids = jnp.concatenate([pos_ids, neg_ids], axis=0)
    owner = ids // labels - lax.axis_index("feat") * owners
    row = iota((owners, 1), 0)
    count = jnp.zeros((owners, docs), F32)
    for slot in range(ids.shape[0]):
        count += jnp.where(owner[slot : slot + 1] == row, 1.0, 0.0)
    before = jnp.where(iota((docs, docs), 0) < iota((docs, docs), 1), 1.0, 0.0).astype(BF16)
    base = jnp.dot(count.astype(BF16), before, preferred_element_type=F32)
    place = jnp.where(count > 0.0, base, -1.0)
    base_ref[...] = base
    pairs_ref[...] = count

    me = lax.axis_index("label")
    own_place = jnp.sum(jnp.where(row == me, place, 0.0), axis=0, keepdims=True)
    name = jnp.where(owner == me, ids % labels + 1, 0).astype(F32).astype(BF16)
    spot = iota((PAIRS + 8, 1), 0)
    rank = spot // 8 * QUARTER + spot % QUARTER + spot % 8 // QUARTER * (PAIRS // 2)
    rank = jnp.where(spot < PAIRS, rank, -2).astype(F32)
    listed = lax.dot_general(one_hot(rank, own_place), name, NT, preferred_element_type=F32)
    names = (iota((1, labels), 1) + 1).astype(F32)
    hits = [
        jnp.where(listed[:, slot : slot + 1] == names, 1.0, 0.0) for slot in range(ids.shape[0])
    ]
    pos_ref[...] = sum(hits[1:pos_slots], hits[0])
    neg_ref[...] = sum(hits[pos_slots + 1 :], hits[pos_slots])


def forward_kernel(
    ids_hbm, used_hbm, pos_hbm, neg_hbm, values_hbm, weight_hbm,
    packed_hbm, count_ref, out_ref, base_ref, pairs_ref, pos_ref, neg_ref,
    ids_ref, used_ref, pos_ids, neg_ids, code_ref, values, weight, rank_ref, stage, total_ref,
    sems, weight_sem, stage_sem, id_sems, *, owners, labels,
):
    groups = values.shape[0]
    blocks, cols, width = weight.shape
    docs = groups * GROUP
    id_loads = [
        pltpu.make_async_copy(ids_hbm, ids_ref, id_sems.at[0]),
        pltpu.make_async_copy(used_hbm, used_ref, id_sems.at[1]),
        pltpu.make_async_copy(pos_hbm, pos_ids, id_sems.at[2]),
        pltpu.make_async_copy(neg_hbm, neg_ids, id_sems.at[3]),
    ]
    for load in id_loads:
        load.start()
    loads = [
        pltpu.make_async_copy(values_hbm.at[g], values.at[g], sems.at[g]) for g in range(groups)
    ]
    for load in loads:
        load.start()
    weight_load = pltpu.make_async_copy(weight_hbm, weight, weight_sem)
    weight_load.start()

    for load in id_loads:
        load.wait()
    slots, _ = ids_ref.shape
    lanes = GROUP * slots
    local = ids_ref[...] - lax.axis_index("feat") * blocks
    inside = (local >= 0) & (local < blocks) & (iota((slots, 1), 0) < used_ref[...].reshape(1, docs))
    ids = jnp.where(inside, local, -1).astype(F32)
    ids = jnp.concatenate([ids[:, g * GROUP : (g + 1) * GROUP] for g in range(groups)], axis=0)
    spread = one_hot(iota((GROUP, lanes), 0), iota((GROUP, lanes), 1) // slots)
    wide = jnp.dot(ids.astype(BF16), spread, preferred_element_type=F32)
    own_slot = iota(wide.shape, 0) % slots == iota(wide.shape, 1) % slots
    wide = jnp.where(own_slot, wide, 0.0).reshape(groups, slots, lanes)
    pad_groups = code_ref.shape[0]
    code_ref[...] = jnp.full(code_ref.shape, -1.0, F32)
    code_ref[:groups] = jnp.sum(wide, axis=1)
    code = code_ref[...]
    listed = jnp.where(code >= 0.0, 1.0, 0.0)
    listed16 = listed.astype(BF16)
    ahead = jnp.where(iota((lanes, lanes), 0) < iota((lanes, lanes), 1), 1.0, 0.0).astype(BF16)
    above = jnp.where(
        iota((pad_groups, pad_groups), 0) > iota((pad_groups, pad_groups), 1), 1.0, 0.0
    ).astype(BF16)
    upper = jnp.dot(above, listed16, preferred_element_type=F32).astype(BF16)
    rank = jnp.dot(listed16, ahead, preferred_element_type=F32) + jnp.dot(
        upper, jnp.ones((lanes, lanes), BF16), preferred_element_type=F32
    )
    rank_ref[...] = jnp.where(code >= 0.0, rank, -1.0)
    count = jnp.sum(listed).astype(jnp.int32)
    chunks = jnp.maximum((count + CHUNK - 1) // CHUNK, 1)
    count_ref[0, 0] = chunks
    name_rows(
        pos_ids[...], neg_ids[...], owners, labels, base_ref, pairs_ref, pos_ref, neg_ref
    )
    note_row = iota((NOTES, lanes), 0)
    lane_doc = (iota((NOTES, lanes), 1) // (lanes // GROUP)).astype(F32)

    def add_chunk(chunk, wait):
        spots = (iota((CHUNK, 1), 0) + chunk * CHUNK).astype(F32)
        rows = jnp.zeros((CHUNK, width), F32)
        notes = jnp.zeros((NOTES, CHUNK), F32)
        for g in range(groups):
            pick = one_hot(spots, rank_ref[g : g + 1])
            told = jnp.where(note_row == 0, code_ref[g : g + 1], 0.0)
            told = jnp.where(note_row == 1, lane_doc, told)
            told = jnp.where(note_row == 2, float(g), told).astype(BF16)
            notes += lax.dot_general(told, pick, NT, preferred_element_type=F32)
            if wait:
                loads[g].wait()
            rows += jnp.dot(pick, values[g], preferred_element_type=F32)
        stage[:CHUNK] = rows.astype(BF16)
        stage[CHUNK:] = notes.astype(BF16)
        save = pltpu.make_async_copy(stage, packed_hbm.at[chunk], stage_sem)
        save.start()
        doc_rows, block = owner_rows(stage[CHUNK:], docs)
        if wait:
            weight_load.wait()
        every = lax.dot_general(
            weight[...].reshape(blocks * cols, width), stage[:CHUNK], NT, preferred_element_type=F32
        )
        part = jnp.zeros((cols, CHUNK), F32)
        for b in range(blocks):
            part += jnp.where(block == float(b), every[b * cols : (b + 1) * cols], 0.0)
        high = part.astype(BF16)
        low = (part - high.astype(F32)).astype(BF16)
        both = lax.dot_general(
            jnp.concatenate([high, low], axis=0), doc_rows, NT, preferred_element_type=F32
        )
        save.wait()
        return both[:cols] + both[cols:]

    total_ref[...] = add_chunk(0, True)

    @pl.when(chunks > 1)
    def _():
        @pl.loop(1, chunks)
        def _(chunk):
            total_ref[...] += add_chunk(chunk, False)

    part = total_ref[...].astype(BF16)
    for shard in range(out_ref.shape[0]):
        out_ref[shard] = part


def forward(ids, used, pos, neg, values, weight_t, shards, owners, labels):
    blocks, cols, width = weight_t.shape
    groups, lanes, _ = values.shape
    docs = groups * GROUP
    most = -(-groups * lanes // CHUNK)
    code_shape = (-(-groups // 8) * 8, lanes)
    return pl.pallas_call(
        functools.partial(forward_kernel, owners=owners, labels=labels),
        out_shape=(
            jax.ShapeDtypeStruct((most, CHUNK + NOTES, width), BF16),
            jax.ShapeDtypeStruct((1, 1), jnp.int32),
            jax.ShapeDtypeStruct((shards, cols, docs), BF16),
            jax.ShapeDtypeStruct((owners, docs), F32),
            jax.ShapeDtypeStruct((owners, docs), F32),
            jax.ShapeDtypeStruct((PAIRS + 8, labels), F32),
            jax.ShapeDtypeStruct((PAIRS + 8, labels), F32),
        ),
        in_specs=[HBM] * 6,
        out_specs=(HBM, SMEM, VMEM, VMEM, VMEM, VMEM, VMEM),
        scratch_shapes=[
            pltpu.VMEM(ids.shape, jnp.int32),
            pltpu.VMEM(used.shape, jnp.int32),
            pltpu.VMEM(pos.shape, jnp.int32),
            pltpu.VMEM(neg.shape, jnp.int32),
            pltpu.VMEM(code_shape, F32),
            pltpu.VMEM(values.shape, BF16),
            pltpu.VMEM(weight_t.shape, BF16),
            pltpu.VMEM(code_shape, F32),
            pltpu.VMEM((CHUNK + NOTES, width), BF16),
            pltpu.VMEM((cols, docs), F32),
            pltpu.SemaphoreType.DMA((groups,)),
            pltpu.SemaphoreType.DMA(()),
            pltpu.SemaphoreType.DMA(()),
            pltpu.SemaphoreType.DMA((4,)),
        ],
        compiler_params=pltpu.CompilerParams(vmem_limit_bytes=62_500_000),
    )(ids, used, pos, neg, values, weight_t)


def backward_kernel(
    count_ref, parts_ref, pre_ref, packed_hbm, out_hbm, stage, grad_ref, total_ref, held, sem, sems
):
    blocks, cols, width = held.shape
    docs = pre_ref.shape[1]
    chunks = count_ref[0, 0]
    first = pltpu.make_async_copy(packed_hbm.at[0], stage, sem)
    first.start()
    hidden_grad = parts_ref[0].astype(F32)
    for shard in range(1, parts_ref.shape[0]):
        hidden_grad += parts_ref[shard].astype(F32)
    pre = pre_ref[...]
    gate = jax.nn.sigmoid(pre)
    grad_ref[...] = (hidden_grad * gate * (1.0 + pre * (1.0 - gate))).astype(BF16)
    first.wait()
    step = blocks // PIECES

    def slot_grads():
        doc_rows, block = owner_rows(stage[CHUNK:], docs)
        return jnp.dot(grad_ref[...], doc_rows, preferred_element_type=F32), block

    def product(grads, block, piece):
        own = [
            jnp.where(block == float(b), grads, 0.0).astype(BF16)
            for b in range(piece * step, (piece + 1) * step)
        ]
        return jnp.dot(
            jnp.concatenate(own, axis=0), stage[:CHUNK], preferred_element_type=F32
        ).reshape(step, cols, width)

    def finish(piece_of):
        saves = []
        for piece in range(PIECES):
            part = pl.ds(piece * step, step)
            held[part] = piece_of(piece).astype(BF16)
            saves.append(pltpu.make_async_copy(held.at[part], out_hbm.at[part], sems.at[piece]))
            saves[-1].start()
        for save in saves:
            save.wait()

    @pl.when(chunks <= 1)
    def _():
        grads, block = slot_grads()
        finish(lambda piece: product(grads, block, piece))

    @pl.when(chunks > 1)
    def _():
        total_ref[...] = jnp.zeros_like(total_ref)

        @pl.loop(0, chunks)
        def _(chunk):
            later = pltpu.make_async_copy(packed_hbm.at[chunk], stage, sem)
            later.start()
            later.wait()
            grads, block = slot_grads()
            for piece in range(PIECES):
                total_ref[pl.ds(piece * step, step)] += product(grads, block, piece)

        finish(lambda piece: total_ref[pl.ds(piece * step, step)])


def backward(count, parts, pre_t, packed, blocks):
    cols, docs = pre_t.shape
    width = packed.shape[2]
    return pl.pallas_call(
        backward_kernel,
        out_shape=jax.ShapeDtypeStruct((blocks, cols, width), BF16),
        in_specs=[SMEM, VMEM, VMEM, HBM],
        out_specs=HBM,
        scratch_shapes=[
            pltpu.VMEM(packed.shape[1:], BF16),
            pltpu.VMEM((cols, docs), BF16),
            pltpu.VMEM((blocks, cols, width), F32),
            pltpu.VMEM((blocks, cols, width), BF16),
            pltpu.SemaphoreType.DMA(()),
            pltpu.SemaphoreType.DMA((PIECES,)),
        ],
        compiler_params=pltpu.CompilerParams(vmem_limit_bytes=16 << 20),
    )(count, parts, pre_t, packed)


def row_picks(place_ref):
    owners, docs = place_ref.shape
    tile = 2 * QUARTER
    within = iota((tile, 1), 0)
    first = within < QUARTER
    rank = (within % QUARTER).astype(F32)
    places = [
        jnp.where(first, place_ref[o : o + 1], place_ref[o + 1 : o + 2]) for o in range(0, owners, 2)
    ]
    picks = []
    for start in (0, PAIRS // 2):
        picks.append(
            jnp.concatenate(
                [
                    jnp.where(p == rank + float(start + offset), 1.0, 0.0)
                    for offset in range(0, PAIRS // 2, QUARTER)
                    for p in places
                ],
                axis=0,
            ).astype(BF16)
        )
    return picks


def read_rows(ref):
    owners, _, lanes = ref.shape
    return [
        [
            jnp.concatenate(
                [ref[o + i, :, at : at + 128].astype(F32) for i in range(2)], axis=0
            )
            for o in range(0, owners, 2)
        ]
        for at in range(0, lanes, 128)
    ]


def write_rows(ref, group, pair, tile):
    at = group * 128
    ref[2 * pair, :, at : at + 128] = tile[:QUARTER].astype(BF16)
    ref[2 * pair + 1, :, at : at + 128] = tile[QUARTER:].astype(BF16)


def swap(tile):
    keep = (iota(tile.shape, 0) < QUARTER) == (iota(tile.shape, 1) < 64)
    return jnp.where(keep, tile, pltpu.roll(pltpu.roll(tile, QUARTER, 0), 64, 1))


def hidden_kernel(parts_ref, place_ref, pre_ref, sent_ref):
    pre = parts_ref[0].astype(F32)
    for shard in range(1, parts_ref.shape[0]):
        pre += parts_ref[shard].astype(F32)
    pre_ref[...] = pre
    hidden = jax.nn.silu(pre).astype(BF16)
    none = jnp.zeros_like(hidden)
    low, high = row_picks(place_ref)
    rows = lax.dot_general(
        low, jnp.concatenate([hidden, none], axis=0), NT, preferred_element_type=F32
    ) + lax.dot_general(
        high, jnp.concatenate([none, hidden], axis=0), NT, preferred_element_type=F32
    )
    pairs = sent_ref.shape[0] // 2
    for index in range(rows.shape[0] // 8):
        write_rows(sent_ref, index // pairs, index % pairs, rows[index * 8 : (index + 1) * 8])


def label_kernel(got_ref, weight_ref, pos_ref, neg_ref, back_ref, rows_ref, grad_ref):
    groups = [jnp.concatenate([swap(t) for t in tiles], axis=1) for tiles in read_rows(got_ref)]
    groups.append(jnp.zeros_like(groups[0]))
    rows = jnp.concatenate(groups, axis=0).astype(BF16)
    rows_ref[...] = rows
    weight = weight_ref[...]
    logit = lax.dot_general(rows, weight, NT, preferred_element_type=F32)
    sig = jax.nn.sigmoid(logit)
    grad_pos = (sig - 1.0).astype(BF16).astype(F32)
    grad_neg = sig.astype(BF16).astype(F32)
    grad = (pos_ref[...] * grad_pos + neg_ref[...] * grad_neg).astype(BF16)
    grad_ref[...] = grad
    terms = jnp.dot(grad, weight, preferred_element_type=F32)
    for group in range(PAIRS // 8):
        for pair in range(back_ref.shape[0] // 2):
            tile = terms[group * 8 : (group + 1) * 8, pair * 128 : (pair + 1) * 128]
            write_rows(back_ref, group, pair, swap(tile))


def collect_kernel(came_ref, place_ref, out_ref):
    came = jnp.concatenate([t for tiles in read_rows(came_ref) for t in tiles], axis=0).astype(BF16)
    cols = out_ref.shape[1]
    low, high = row_picks(place_ref)
    tn = (((0,), (0,)), ((), ()))
    part = (
        lax.dot_general(came, low, tn, preferred_element_type=F32)[:cols]
        + lax.dot_general(came, high, tn, preferred_element_type=F32)[cols:]
    ).astype(BF16)
    for shard in range(out_ref.shape[0]):
        out_ref[shard] = part


def local_call(kernel, inputs, *shapes):
    return pl.pallas_call(
        kernel,
        out_shape=tuple(jax.ShapeDtypeStruct(shape, kind) for shape, kind in shapes),
        in_specs=[VMEM] * len(inputs),
        out_specs=(VMEM,) * len(shapes),
        compiler_params=pltpu.CompilerParams(vmem_limit_bytes=16 << 20),
    )(*inputs)


def on_device(doc_blocks, doc_counts, doc_values, pos_labels, neg_labels, in_weight, out_weight):
    block_count, block_size, col_count = in_weight.shape
    doc_total, slot_count = doc_blocks.shape
    lab_count, hidden_width = out_weight.shape
    owners = lax.axis_size("label")
    shards = lax.axis_size("feat")
    groups = doc_total // GROUP
    packed, chunks, copies, base, pairs, pos_count, neg_count = forward(
        doc_blocks.T,
        doc_counts,
        pos_labels.T,
        neg_labels.T,
        doc_values.reshape(groups, GROUP * slot_count, block_size),
        jnp.swapaxes(in_weight, 1, 2),
        shards,
        owners,
        lab_count,
    )
    place = jnp.where(pairs > 0, base, -1.0)
    arrived = lax.all_to_all(copies, "feat", 0, 0, tiled=True)
    row_shape = (owners, QUARTER, PAIRS * col_count // QUARTER)
    pre_t, sent = local_call(
        hidden_kernel, (arrived, place), (copies.shape[1:], F32), (row_shape, BF16)
    )
    got = lax.all_to_all(sent, "label", 0, 0, tiled=True)
    back, rows, label_grad = local_call(
        label_kernel,
        (got, out_weight, pos_count, neg_count),
        (row_shape, BF16),
        ((PAIRS + 8, hidden_width), BF16),
        ((PAIRS + 8, lab_count), BF16),
    )
    came = lax.all_to_all(back, "label", 0, 0, tiled=True)
    (copies,) = local_call(collect_kernel, (came, place), (copies.shape, BF16))
    parts = lax.all_to_all(copies, "feat", 0, 0, tiled=True)
    out_grad = lax.dot_general(
        label_grad, rows, (((0,), (0,)), ((), ())), preferred_element_type=F32
    ).astype(BF16)
    in_grad = backward(chunks, parts, pre_t, packed, block_count)
    return (jnp.swapaxes(in_grad, 1, 2), out_grad)


def solution(mesh):
    placed = (P(), P(), P(), P(), P(), P("feat", None, "label"), P(("feat", "label"), None))
    return jax.shard_map(
        on_device,
        mesh=mesh,
        in_specs=placed,
        out_specs=(P("feat", None, "label"), P(("feat", "label"), None)),
        check_vma=False,
    )
```

```python
import functools

import jax
import jax.numpy as jnp
from jax import lax
from jax.experimental import pallas as pl
from jax.experimental.pallas import tpu as pltpu
from jax.sharding import PartitionSpec as P

F32 = jnp.float32
BF16 = jnp.bfloat16
PAIRS = 24
QUARTER = 4


GROUP = 32
CHUNK = 256
NOTES = 16
PIECES = 4
VMEM = pl.BlockSpec(memory_space=pltpu.VMEM)
SMEM = pl.BlockSpec(memory_space=pltpu.SMEM)
HBM = pl.BlockSpec(memory_space=pltpu.HBM)
NT = (((1,), (1,)), ((), ()))


def iota(shape, dim):
    return lax.broadcasted_iota(jnp.int32, shape, dim)


def one_hot(left, right):
    return jnp.where(left == right, 1.0, 0.0).astype(BF16)


def owner_rows(notes, docs):
    held = notes.astype(F32)
    doc = held[2:3] * float(GROUP) + held[1:2]
    return one_hot(iota((docs, 1), 0).astype(F32), doc), held[0:1]


def name_rows(pos_ids, neg_ids, owners, labels, base_ref, pairs_ref, pos_ref, neg_ref):
    pos_slots, docs = pos_ids.shape
    ids = jnp.concatenate([pos_ids, neg_ids], axis=0)
    owner = ids // labels - lax.axis_index("feat") * owners
    row = iota((owners, 1), 0)
    count = jnp.zeros((owners, docs), F32)
    for slot in range(ids.shape[0]):
        count += jnp.where(owner[slot : slot + 1] == row, 1.0, 0.0)
    before = jnp.where(iota((docs, docs), 0) < iota((docs, docs), 1), 1.0, 0.0).astype(BF16)
    base = jnp.dot(count.astype(BF16), before, preferred_element_type=F32)
    place = jnp.where(count > 0.0, base, -1.0)
    base_ref[...] = base
    pairs_ref[...] = count

    me = lax.axis_index("label")
    own_place = jnp.sum(jnp.where(row == me, place, 0.0), axis=0, keepdims=True)
    name = jnp.where(owner == me, ids % labels + 1, 0).astype(F32).astype(BF16)
    spot = iota((PAIRS + 8, 1), 0)
    rank = spot // 8 * QUARTER + spot % QUARTER + spot % 8 // QUARTER * (PAIRS // 2)
    rank = jnp.where(spot < PAIRS, rank, -2).astype(F32)
    listed = lax.dot_general(one_hot(rank, own_place), name, NT, preferred_element_type=F32)
    names = (iota((1, labels), 1) + 1).astype(F32)
    hits = [
        jnp.where(listed[:, slot : slot + 1] == names, 1.0, 0.0) for slot in range(ids.shape[0])
    ]
    pos_ref[...] = sum(hits[1:pos_slots], hits[0])
    neg_ref[...] = sum(hits[pos_slots + 1 :], hits[pos_slots])


def forward_kernel(
    ids_hbm, used_hbm, pos_hbm, neg_hbm, values_hbm, weight_hbm,
    packed_hbm, first_ref, count_ref, out_ref, base_ref, pairs_ref, pos_ref, neg_ref,
    ids_ref, used_ref, pos_ids, neg_ids, code_ref, values, weight, rank_ref, stage, total_ref,
    values_sem, weight_sem, stage_sem, id_sems, *, owners, labels,
):
    groups = values.shape[0]
    blocks, cols, width = weight.shape
    docs = groups * GROUP
    id_loads = [
        pltpu.make_async_copy(ids_hbm, ids_ref, id_sems.at[0]),
        pltpu.make_async_copy(used_hbm, used_ref, id_sems.at[1]),
        pltpu.make_async_copy(pos_hbm, pos_ids, id_sems.at[2]),
        pltpu.make_async_copy(neg_hbm, neg_ids, id_sems.at[3]),
    ]
    for id_load in id_loads:
        id_load.start()
    load = pltpu.make_async_copy(values_hbm, values, values_sem)
    load.start()
    weight_load = pltpu.make_async_copy(weight_hbm, weight, weight_sem)
    weight_load.start()

    for id_load in id_loads:
        id_load.wait()
    slots, _ = ids_ref.shape
    lanes = GROUP * slots
    local = ids_ref[...] - lax.axis_index("feat") * blocks
    inside = (local >= 0) & (local < blocks) & (iota((slots, 1), 0) < used_ref[...].reshape(1, docs))
    ids = jnp.where(inside, local, -1).astype(F32)
    ids = jnp.concatenate([ids[:, g * GROUP : (g + 1) * GROUP] for g in range(groups)], axis=0)
    spread = one_hot(iota((GROUP, lanes), 0), iota((GROUP, lanes), 1) // slots)
    wide = jnp.dot(ids.astype(BF16), spread, preferred_element_type=F32)
    own_slot = iota(wide.shape, 0) % slots == iota(wide.shape, 1) % slots
    wide = jnp.where(own_slot, wide, 0.0).reshape(groups, slots, lanes)
    pad_groups = code_ref.shape[0]
    code_ref[...] = jnp.full(code_ref.shape, -1.0, F32)
    code_ref[:groups] = jnp.sum(wide, axis=1)
    code = code_ref[...]
    listed = jnp.where(code >= 0.0, 1.0, 0.0)
    listed16 = listed.astype(BF16)
    ahead = jnp.where(iota((lanes, lanes), 0) < iota((lanes, lanes), 1), 1.0, 0.0).astype(BF16)
    above = jnp.where(
        iota((pad_groups, pad_groups), 0) > iota((pad_groups, pad_groups), 1), 1.0, 0.0
    ).astype(BF16)
    upper = jnp.dot(above, listed16, preferred_element_type=F32).astype(BF16)
    rank = jnp.dot(listed16, ahead, preferred_element_type=F32) + jnp.dot(
        upper, jnp.ones((lanes, lanes), BF16), preferred_element_type=F32
    )
    rank_ref[...] = jnp.where(code >= 0.0, rank, -1.0)
    count = jnp.sum(listed).astype(jnp.int32)
    chunks = jnp.maximum((count + CHUNK - 1) // CHUNK, 1)
    count_ref[0, 0] = chunks
    name_rows(
        pos_ids[...], neg_ids[...], owners, labels, base_ref, pairs_ref, pos_ref, neg_ref
    )
    note_row = iota((NOTES, lanes), 0)
    lane_doc = (iota((NOTES, lanes), 1) // (lanes // GROUP)).astype(F32)

    def add_chunk(chunk, stage, wait):
        spots = (iota((CHUNK, 1), 0) + chunk * CHUNK).astype(F32)
        if wait:
            load.wait()
        rows = jnp.zeros((CHUNK, width), F32)
        notes = jnp.zeros((NOTES, CHUNK), F32)
        for g in range(groups):
            pick = one_hot(spots, rank_ref[g : g + 1])
            told = jnp.where(note_row == 0, code_ref[g : g + 1], 0.0)
            told = jnp.where(note_row == 1, lane_doc, told)
            told = jnp.where(note_row == 2, float(g), told).astype(BF16)
            notes += lax.dot_general(told, pick, NT, preferred_element_type=F32)
            rows += jnp.dot(pick, values[g], preferred_element_type=F32)
        stage[:CHUNK] = rows.astype(BF16)
        stage[CHUNK:] = notes.astype(BF16)
        doc_rows, block = owner_rows(stage[CHUNK:], docs)
        if wait:
            weight_load.wait()
        every = lax.dot_general(
            weight[...].reshape(blocks * cols, width), stage[:CHUNK], NT, preferred_element_type=F32
        )
        part = jnp.zeros((cols, CHUNK), F32)
        for b in range(blocks):
            part += jnp.where(block == float(b), every[b * cols : (b + 1) * cols], 0.0)
        high = part.astype(BF16)
        low = (part - high.astype(F32)).astype(BF16)
        both = lax.dot_general(
            jnp.concatenate([high, low], axis=0), doc_rows, NT, preferred_element_type=F32
        )
        return both[:cols] + both[cols:]

    total_ref[...] = add_chunk(0, first_ref, True)

    @pl.when(chunks > 1)
    def _():
        @pl.loop(1, chunks)
        def _(chunk):
            total_ref[...] += add_chunk(chunk, stage, False)
            save = pltpu.make_async_copy(stage, packed_hbm.at[chunk - 1], stage_sem)
            save.start()
            save.wait()

    part = total_ref[...].astype(BF16)
    for shard in range(out_ref.shape[0]):
        out_ref[shard] = part


def forward(ids, used, pos, neg, values, weight_t, shards, owners, labels):
    blocks, cols, width = weight_t.shape
    groups, lanes, _ = values.shape
    docs = groups * GROUP
    most = -(-groups * lanes // CHUNK)
    code_shape = (-(-groups // 8) * 8, lanes)
    return pl.pallas_call(
        functools.partial(forward_kernel, owners=owners, labels=labels),
        out_shape=(
            jax.ShapeDtypeStruct((most - 1, CHUNK + NOTES, width), BF16),
            jax.ShapeDtypeStruct((CHUNK + NOTES, width), BF16),
            jax.ShapeDtypeStruct((1, 1), jnp.int32),
            jax.ShapeDtypeStruct((shards, cols, docs), BF16),
            jax.ShapeDtypeStruct((owners, docs), F32),
            jax.ShapeDtypeStruct((owners, docs), F32),
            jax.ShapeDtypeStruct((PAIRS + 8, labels), F32),
            jax.ShapeDtypeStruct((PAIRS + 8, labels), F32),
        ),
        in_specs=[HBM] * 6,
        out_specs=(HBM, VMEM, SMEM, VMEM, VMEM, VMEM, VMEM, VMEM),
        scratch_shapes=[
            pltpu.VMEM(ids.shape, jnp.int32),
            pltpu.VMEM(used.shape, jnp.int32),
            pltpu.VMEM(pos.shape, jnp.int32),
            pltpu.VMEM(neg.shape, jnp.int32),
            pltpu.VMEM(code_shape, F32),
            pltpu.VMEM(values.shape, BF16),
            pltpu.VMEM(weight_t.shape, BF16),
            pltpu.VMEM(code_shape, F32),
            pltpu.VMEM((CHUNK + NOTES, width), BF16),
            pltpu.VMEM((cols, docs), F32),
            pltpu.SemaphoreType.DMA(()),
            pltpu.SemaphoreType.DMA(()),
            pltpu.SemaphoreType.DMA(()),
            pltpu.SemaphoreType.DMA((4,)),
        ],
        compiler_params=pltpu.CompilerParams(vmem_limit_bytes=62_500_000),
    )(ids, used, pos, neg, values, weight_t)


def backward_kernel(
    count_ref, parts_ref, pre_ref, first_ref, packed_hbm, out_hbm, stage, grad_ref, total_ref, held, sem, sems
):
    blocks, cols, width = held.shape
    docs = pre_ref.shape[1]
    chunks = count_ref[0, 0]
    hidden_grad = parts_ref[0].astype(F32)
    for shard in range(1, parts_ref.shape[0]):
        hidden_grad += parts_ref[shard].astype(F32)
    pre = pre_ref[...]
    gate = jax.nn.sigmoid(pre)
    grad_ref[...] = (hidden_grad * gate * (1.0 + pre * (1.0 - gate))).astype(BF16)
    step = blocks // PIECES

    def slot_grads(stage):
        doc_rows, block = owner_rows(stage[CHUNK:], docs)
        return jnp.dot(grad_ref[...], doc_rows, preferred_element_type=F32), block

    def product(stage, grads, block, piece):
        own = [
            jnp.where(block == float(b), grads, 0.0).astype(BF16)
            for b in range(piece * step, (piece + 1) * step)
        ]
        return jnp.dot(
            jnp.concatenate(own, axis=0), stage[:CHUNK], preferred_element_type=F32
        ).reshape(step, cols, width)

    def finish(piece_of):
        saves = []
        for piece in range(PIECES):
            part = pl.ds(piece * step, step)
            held[part] = piece_of(piece).astype(BF16)
            saves.append(pltpu.make_async_copy(held.at[part], out_hbm.at[part], sems.at[piece]))
            saves[-1].start()
        for save in saves:
            save.wait()

    @pl.when(chunks <= 1)
    def _():
        grads, block = slot_grads(first_ref)
        finish(lambda piece: product(first_ref, grads, block, piece))

    @pl.when(chunks > 1)
    def _():
        def add(stage):
            grads, block = slot_grads(stage)
            for piece in range(PIECES):
                total_ref[pl.ds(piece * step, step)] += product(stage, grads, block, piece)

        total_ref[...] = jnp.zeros_like(total_ref)
        add(first_ref)

        @pl.loop(1, chunks)
        def _(chunk):
            later = pltpu.make_async_copy(packed_hbm.at[chunk - 1], stage, sem)
            later.start()
            later.wait()
            add(stage)

        finish(lambda piece: total_ref[pl.ds(piece * step, step)])


def backward(count, parts, pre_t, first, packed, blocks):
    cols, docs = pre_t.shape
    width = packed.shape[2]
    return pl.pallas_call(
        backward_kernel,
        out_shape=jax.ShapeDtypeStruct((blocks, cols, width), BF16),
        in_specs=[SMEM, VMEM, VMEM, VMEM, HBM],
        out_specs=HBM,
        scratch_shapes=[
            pltpu.VMEM(packed.shape[1:], BF16),
            pltpu.VMEM((cols, docs), BF16),
            pltpu.VMEM((blocks, cols, width), F32),
            pltpu.VMEM((blocks, cols, width), BF16),
            pltpu.SemaphoreType.DMA(()),
            pltpu.SemaphoreType.DMA((PIECES,)),
        ],
        compiler_params=pltpu.CompilerParams(vmem_limit_bytes=16 << 20),
    )(count, parts, pre_t, first, packed)


def row_picks(place_ref):
    owners, docs = place_ref.shape
    tile = 2 * QUARTER
    within = iota((tile, 1), 0)
    first = within < QUARTER
    rank = (within % QUARTER).astype(F32)
    places = [
        jnp.where(first, place_ref[o : o + 1], place_ref[o + 1 : o + 2]) for o in range(0, owners, 2)
    ]
    picks = []
    for start in (0, PAIRS // 2):
        picks.append(
            jnp.concatenate(
                [
                    jnp.where(p == rank + float(start + offset), 1.0, 0.0)
                    for offset in range(0, PAIRS // 2, QUARTER)
                    for p in places
                ],
                axis=0,
            ).astype(BF16)
        )
    return picks


def read_rows(ref):
    owners, _, lanes = ref.shape
    return [
        [
            jnp.concatenate(
                [ref[o + i, :, at : at + 128].astype(F32) for i in range(2)], axis=0
            )
            for o in range(0, owners, 2)
        ]
        for at in range(0, lanes, 128)
    ]


def write_rows(ref, group, pair, tile):
    at = group * 128
    ref[2 * pair, :, at : at + 128] = tile[:QUARTER].astype(BF16)
    ref[2 * pair + 1, :, at : at + 128] = tile[QUARTER:].astype(BF16)


def swap(tile):
    keep = (iota(tile.shape, 0) < QUARTER) == (iota(tile.shape, 1) < 64)
    return jnp.where(keep, tile, pltpu.roll(pltpu.roll(tile, QUARTER, 0), 64, 1))


def hidden_kernel(parts_ref, place_ref, pre_ref, sent_ref):
    pre = parts_ref[0].astype(F32)
    for shard in range(1, parts_ref.shape[0]):
        pre += parts_ref[shard].astype(F32)
    pre_ref[...] = pre
    hidden = jax.nn.silu(pre).astype(BF16)
    none = jnp.zeros_like(hidden)
    low, high = row_picks(place_ref)
    rows = lax.dot_general(
        low, jnp.concatenate([hidden, none], axis=0), NT, preferred_element_type=F32
    ) + lax.dot_general(
        high, jnp.concatenate([none, hidden], axis=0), NT, preferred_element_type=F32
    )
    pairs = sent_ref.shape[0] // 2
    for index in range(rows.shape[0] // 8):
        write_rows(sent_ref, index // pairs, index % pairs, rows[index * 8 : (index + 1) * 8])


def label_kernel(got_ref, weight_ref, pos_ref, neg_ref, back_ref, rows_ref, grad_ref):
    groups = [jnp.concatenate([swap(t) for t in tiles], axis=1) for tiles in read_rows(got_ref)]
    groups.append(jnp.zeros_like(groups[0]))
    rows = jnp.concatenate(groups, axis=0).astype(BF16)
    rows_ref[...] = rows
    weight = weight_ref[...]
    logit = lax.dot_general(rows, weight, NT, preferred_element_type=F32)
    sig = jax.nn.sigmoid(logit)
    grad_pos = (sig - 1.0).astype(BF16).astype(F32)
    grad_neg = sig.astype(BF16).astype(F32)
    grad = (pos_ref[...] * grad_pos + neg_ref[...] * grad_neg).astype(BF16)
    grad_ref[...] = grad
    terms = jnp.dot(grad, weight, preferred_element_type=F32)
    for group in range(PAIRS // 8):
        for pair in range(back_ref.shape[0] // 2):
            tile = terms[group * 8 : (group + 1) * 8, pair * 128 : (pair + 1) * 128]
            write_rows(back_ref, group, pair, swap(tile))


def collect_kernel(came_ref, place_ref, out_ref):
    came = jnp.concatenate([t for tiles in read_rows(came_ref) for t in tiles], axis=0).astype(BF16)
    cols = out_ref.shape[1]
    low, high = row_picks(place_ref)
    tn = (((0,), (0,)), ((), ()))
    part = (
        lax.dot_general(came, low, tn, preferred_element_type=F32)[:cols]
        + lax.dot_general(came, high, tn, preferred_element_type=F32)[cols:]
    ).astype(BF16)
    for shard in range(out_ref.shape[0]):
        out_ref[shard] = part


def local_call(kernel, inputs, *shapes):
    return pl.pallas_call(
        kernel,
        out_shape=tuple(jax.ShapeDtypeStruct(shape, kind) for shape, kind in shapes),
        in_specs=[VMEM] * len(inputs),
        out_specs=(VMEM,) * len(shapes),
        compiler_params=pltpu.CompilerParams(vmem_limit_bytes=16 << 20),
    )(*inputs)


def on_device(doc_blocks, doc_counts, doc_values, pos_labels, neg_labels, in_weight, out_weight):
    block_count, block_size, col_count = in_weight.shape
    doc_total, slot_count = doc_blocks.shape
    lab_count, hidden_width = out_weight.shape
    owners = lax.axis_size("label")
    shards = lax.axis_size("feat")
    groups = doc_total // GROUP
    packed, first, chunks, copies, base, pairs, pos_count, neg_count = forward(
        doc_blocks.T,
        doc_counts,
        pos_labels.T,
        neg_labels.T,
        doc_values.reshape(groups, GROUP * slot_count, block_size),
        jnp.swapaxes(in_weight, 1, 2),
        shards,
        owners,
        lab_count,
    )
    place = jnp.where(pairs > 0, base, -1.0)
    arrived = lax.all_to_all(copies, "feat", 0, 0, tiled=True)
    row_shape = (owners, QUARTER, PAIRS * col_count // QUARTER)
    pre_t, sent = local_call(
        hidden_kernel, (arrived, place), (copies.shape[1:], F32), (row_shape, BF16)
    )
    got = lax.all_to_all(sent, "label", 0, 0, tiled=True)
    back, rows, label_grad = local_call(
        label_kernel,
        (got, out_weight, pos_count, neg_count),
        (row_shape, BF16),
        ((PAIRS + 8, hidden_width), BF16),
        ((PAIRS + 8, lab_count), BF16),
    )
    came = lax.all_to_all(back, "label", 0, 0, tiled=True)
    (copies,) = local_call(collect_kernel, (came, place), (copies.shape, BF16))
    parts = lax.all_to_all(copies, "feat", 0, 0, tiled=True)
    out_grad = lax.dot_general(
        label_grad, rows, (((0,), (0,)), ((), ())), preferred_element_type=F32
    ).astype(BF16)
    in_grad = backward(chunks, parts, pre_t, first, packed, block_count)
    return (jnp.swapaxes(in_grad, 1, 2), out_grad)


def solution(mesh):
    placed = (P(), P(), P(), P(), P(), P("feat", None, "label"), P(("feat", "label"), None))
    return jax.shard_map(
        on_device,
        mesh=mesh,
        in_specs=placed,
        out_specs=(P("feat", None, "label"), P(("feat", "label"), None)),
        check_vma=False,
    )
```

```python
import functools

import jax
import jax.numpy as jnp
from jax import lax
from jax.experimental import pallas as pl
from jax.experimental.pallas import tpu as pltpu
from jax.sharding import PartitionSpec as P

F32 = jnp.float32
BF16 = jnp.bfloat16
PAIRS = 24
QUARTER = 4


GROUP = 32
CHUNK = 256
NOTES = 16
PIECES = 4
VMEM = pl.BlockSpec(memory_space=pltpu.VMEM)
SMEM = pl.BlockSpec(memory_space=pltpu.SMEM)
HBM = pl.BlockSpec(memory_space=pltpu.HBM)
NT = (((1,), (1,)), ((), ()))


def iota(shape, dim):
    return lax.broadcasted_iota(jnp.int32, shape, dim)


def one_hot(left, right):
    return jnp.where(left == right, 1.0, 0.0).astype(BF16)


def owner_rows(notes, docs):
    held = notes.astype(F32)
    doc = held[2:3] * float(GROUP) + held[1:2]
    return one_hot(iota((docs, 1), 0).astype(F32), doc), held[0:1]


def name_rows(pos_ids, neg_ids, owners, labels, base_ref, pairs_ref, pos_ref, neg_ref):
    pos_slots, docs = pos_ids.shape
    ids = jnp.concatenate([pos_ids, neg_ids], axis=0)
    owner = ids // labels - lax.axis_index("feat") * owners
    row = iota((owners, 1), 0)
    count = jnp.zeros((owners, docs), F32)
    for slot in range(ids.shape[0]):
        count += jnp.where(owner[slot : slot + 1] == row, 1.0, 0.0)
    before = jnp.where(iota((docs, docs), 0) < iota((docs, docs), 1), 1.0, 0.0).astype(BF16)
    base = jnp.dot(count.astype(BF16), before, preferred_element_type=F32)
    place = jnp.where(count > 0.0, base, -1.0)
    base_ref[...] = base
    pairs_ref[...] = count

    me = lax.axis_index("label")
    own_place = jnp.sum(jnp.where(row == me, place, 0.0), axis=0, keepdims=True)
    name = jnp.where(owner == me, ids % labels + 1, 0).astype(F32).astype(BF16)
    spot = iota((PAIRS + 8, 1), 0)
    rank = spot // 8 * QUARTER + spot % QUARTER + spot % 8 // QUARTER * (PAIRS // 2)
    rank = jnp.where(spot < PAIRS, rank, -2).astype(F32)
    listed = lax.dot_general(one_hot(rank, own_place), name, NT, preferred_element_type=F32)
    names = (iota((1, labels), 1) + 1).astype(F32)
    hits = [
        jnp.where(listed[:, slot : slot + 1] == names, 1.0, 0.0) for slot in range(ids.shape[0])
    ]
    pos_ref[...] = sum(hits[1:pos_slots], hits[0])
    neg_ref[...] = sum(hits[pos_slots + 1 :], hits[pos_slots])


def forward_kernel(
    ids_hbm, used_hbm, pos_hbm, neg_hbm, values_hbm, weight_hbm,
    packed_hbm, first_ref, count_ref, out_ref, base_ref, pairs_ref, pos_ref, neg_ref,
    ids_ref, used_ref, pos_ids, neg_ids, code_ref, values, weight, rank_ref, stage, total_ref,
    values_sem, weight_sem, stage_sem, id_sems, *, owners, labels,
):
    groups = values.shape[0]
    blocks, cols, width = weight.shape
    docs = groups * GROUP
    id_loads = [
        pltpu.make_async_copy(ids_hbm, ids_ref, id_sems.at[0]),
        pltpu.make_async_copy(used_hbm, used_ref, id_sems.at[1]),
        pltpu.make_async_copy(pos_hbm, pos_ids, id_sems.at[2]),
        pltpu.make_async_copy(neg_hbm, neg_ids, id_sems.at[3]),
    ]
    for id_load in id_loads:
        id_load.start()
    load = pltpu.make_async_copy(values_hbm, values, values_sem)
    load.start()
    weight_load = pltpu.make_async_copy(weight_hbm, weight, weight_sem)
    weight_load.start()

    for id_load in id_loads:
        id_load.wait()
    slots, _ = ids_ref.shape
    lanes = GROUP * slots
    local = ids_ref[...] - lax.axis_index("feat") * blocks
    inside = (local >= 0) & (local < blocks) & (iota((slots, 1), 0) < used_ref[...].reshape(1, docs))
    ids = jnp.where(inside, local, -1).astype(F32)
    ids = jnp.concatenate([ids[:, g * GROUP : (g + 1) * GROUP] for g in range(groups)], axis=0)
    spread = one_hot(iota((GROUP, lanes), 0), iota((GROUP, lanes), 1) // slots)
    wide = jnp.dot(ids.astype(BF16), spread, preferred_element_type=F32)
    own_slot = iota(wide.shape, 0) % slots == iota(wide.shape, 1) % slots
    wide = jnp.where(own_slot, wide, 0.0).reshape(groups, slots, lanes)
    pad_groups = code_ref.shape[0]
    code_ref[...] = jnp.full(code_ref.shape, -1.0, F32)
    code_ref[:groups] = jnp.sum(wide, axis=1)
    code = code_ref[...]
    listed = jnp.where(code >= 0.0, 1.0, 0.0)
    listed16 = listed.astype(BF16)
    ahead = jnp.where(iota((lanes, lanes), 0) < iota((lanes, lanes), 1), 1.0, 0.0).astype(BF16)
    above = jnp.where(
        iota((pad_groups, pad_groups), 0) > iota((pad_groups, pad_groups), 1), 1.0, 0.0
    ).astype(BF16)
    upper = jnp.dot(above, listed16, preferred_element_type=F32).astype(BF16)
    rank = jnp.dot(listed16, ahead, preferred_element_type=F32) + jnp.dot(
        upper, jnp.ones((lanes, lanes), BF16), preferred_element_type=F32
    )
    rank_ref[...] = jnp.where(code >= 0.0, rank, -1.0)
    count = jnp.sum(listed).astype(jnp.int32)
    chunks = jnp.maximum((count + CHUNK - 1) // CHUNK, 1)
    count_ref[0, 0] = chunks
    name_rows(
        pos_ids[...], neg_ids[...], owners, labels, base_ref, pairs_ref, pos_ref, neg_ref
    )
    note_row = iota((NOTES, lanes), 0)
    lane_doc = (iota((NOTES, lanes), 1) // (lanes // GROUP)).astype(F32)

    def add_chunk(chunk, stage, wait):
        spots = (iota((CHUNK, 1), 0) + chunk * CHUNK).astype(F32)
        if wait:
            load.wait()
        rows = jnp.zeros((CHUNK, width), F32)
        notes = jnp.zeros((NOTES, CHUNK), F32)
        for g in range(groups):
            pick = one_hot(spots, rank_ref[g : g + 1])
            told = jnp.where(note_row == 0, code_ref[g : g + 1], 0.0)
            told = jnp.where(note_row == 1, lane_doc, told)
            told = jnp.where(note_row == 2, float(g), told).astype(BF16)
            notes += lax.dot_general(told, pick, NT, preferred_element_type=F32)
            rows += jnp.dot(pick, values[g], preferred_element_type=F32)
        stage[:CHUNK] = rows.astype(BF16)
        stage[CHUNK:] = notes.astype(BF16)
        doc_rows, block = owner_rows(stage[CHUNK:], docs)
        if wait:
            weight_load.wait()
        every = lax.dot_general(
            weight[...].reshape(blocks * cols, width), stage[:CHUNK], NT, preferred_element_type=F32
        )
        part = jnp.zeros((cols, CHUNK), F32)
        for b in range(blocks):
            part += jnp.where(block == float(b), every[b * cols : (b + 1) * cols], 0.0)
        high = part.astype(BF16)
        low = (part - high.astype(F32)).astype(BF16)
        both = lax.dot_general(
            jnp.concatenate([high, low], axis=0), doc_rows, NT, preferred_element_type=F32
        )
        return both[:cols] + both[cols:]

    total_ref[...] = add_chunk(0, first_ref, True)

    @pl.when(chunks > 1)
    def _():
        @pl.loop(1, chunks)
        def _(chunk):
            total_ref[...] += add_chunk(chunk, stage, False)
            save = pltpu.make_async_copy(stage, packed_hbm.at[chunk - 1], stage_sem)
            save.start()
            save.wait()

    part = total_ref[...].astype(BF16)
    for shard in range(out_ref.shape[0]):
        out_ref[shard] = part


def forward(ids, used, pos, neg, values, weight_t, shards, owners, labels):
    blocks, cols, width = weight_t.shape
    groups, lanes, _ = values.shape
    docs = groups * GROUP
    most = -(-groups * lanes // CHUNK)
    code_shape = (-(-groups // 8) * 8, lanes)
    return pl.pallas_call(
        functools.partial(forward_kernel, owners=owners, labels=labels),
        out_shape=(
            jax.ShapeDtypeStruct((most - 1, CHUNK + NOTES, width), BF16),
            jax.ShapeDtypeStruct((CHUNK + NOTES, width), BF16),
            jax.ShapeDtypeStruct((1, 1), jnp.int32),
            jax.ShapeDtypeStruct((shards, cols, docs), BF16),
            jax.ShapeDtypeStruct((owners, docs), F32),
            jax.ShapeDtypeStruct((owners, docs), F32),
            jax.ShapeDtypeStruct((PAIRS + 8, labels), F32),
            jax.ShapeDtypeStruct((PAIRS + 8, labels), F32),
        ),
        in_specs=[HBM] * 6,
        out_specs=(HBM, VMEM, SMEM, VMEM, VMEM, VMEM, VMEM, VMEM),
        scratch_shapes=[
            pltpu.VMEM(ids.shape, jnp.int32),
            pltpu.VMEM(used.shape, jnp.int32),
            pltpu.VMEM(pos.shape, jnp.int32),
            pltpu.VMEM(neg.shape, jnp.int32),
            pltpu.VMEM(code_shape, F32),
            pltpu.VMEM(values.shape, BF16),
            pltpu.VMEM(weight_t.shape, BF16),
            pltpu.VMEM(code_shape, F32),
            pltpu.VMEM((CHUNK + NOTES, width), BF16),
            pltpu.VMEM((cols, docs), F32),
            pltpu.SemaphoreType.DMA(()),
            pltpu.SemaphoreType.DMA(()),
            pltpu.SemaphoreType.DMA(()),
            pltpu.SemaphoreType.DMA((4,)),
        ],
        compiler_params=pltpu.CompilerParams(vmem_limit_bytes=62_500_000),
    )(ids, used, pos, neg, values, weight_t)


def backward_kernel(
    count_ref, parts_ref, pre_ref, first_ref, packed_hbm, out_hbm, stage, grad_ref, total_ref, held, sem, sems
):
    blocks, cols, width = held.shape
    docs = pre_ref.shape[1]
    chunks = count_ref[0, 0]
    hidden_grad = parts_ref[0].astype(F32)
    for shard in range(1, parts_ref.shape[0]):
        hidden_grad += parts_ref[shard].astype(F32)
    pre = pre_ref[...]
    gate = jax.nn.sigmoid(pre)
    grad_ref[...] = (hidden_grad * gate * (1.0 + pre * (1.0 - gate))).astype(BF16)
    step = blocks // PIECES

    def slot_grads(stage):
        doc_rows, block = owner_rows(stage[CHUNK:], docs)
        return jnp.dot(grad_ref[...], doc_rows, preferred_element_type=F32), block

    def product(stage, grads, block, piece):
        own = [
            jnp.where(block == float(b), grads, 0.0).astype(BF16)
            for b in range(piece * step, (piece + 1) * step)
        ]
        return jnp.dot(
            jnp.concatenate(own, axis=0), stage[:CHUNK], preferred_element_type=F32
        ).reshape(step, cols, width)

    def finish(piece_of):
        saves = []
        for piece in range(PIECES):
            part = pl.ds(piece * step, step)
            held[part] = piece_of(piece).astype(BF16)
            saves.append(pltpu.make_async_copy(held.at[part], out_hbm.at[part], sems.at[piece]))
            saves[-1].start()
        for save in saves:
            save.wait()

    @pl.when(chunks <= 1)
    def _():
        grads, block = slot_grads(first_ref)
        finish(lambda piece: product(first_ref, grads, block, piece))

    @pl.when(chunks > 1)
    def _():
        def add(stage):
            grads, block = slot_grads(stage)
            for piece in range(PIECES):
                total_ref[pl.ds(piece * step, step)] += product(stage, grads, block, piece)

        total_ref[...] = jnp.zeros_like(total_ref)
        add(first_ref)

        @pl.loop(1, chunks)
        def _(chunk):
            later = pltpu.make_async_copy(packed_hbm.at[chunk - 1], stage, sem)
            later.start()
            later.wait()
            add(stage)

        finish(lambda piece: total_ref[pl.ds(piece * step, step)])


def backward(count, parts, pre_t, first, packed, blocks):
    cols, docs = pre_t.shape
    width = packed.shape[2]
    return pl.pallas_call(
        backward_kernel,
        out_shape=jax.ShapeDtypeStruct((blocks, cols, width), BF16),
        in_specs=[SMEM, VMEM, VMEM, VMEM, HBM],
        out_specs=HBM,
        scratch_shapes=[
            pltpu.VMEM(packed.shape[1:], BF16),
            pltpu.VMEM((cols, docs), BF16),
            pltpu.VMEM((blocks, cols, width), F32),
            pltpu.VMEM((blocks, cols, width), BF16),
            pltpu.SemaphoreType.DMA(()),
            pltpu.SemaphoreType.DMA((PIECES,)),
        ],
        compiler_params=pltpu.CompilerParams(vmem_limit_bytes=16 << 20),
    )(count, parts, pre_t, first, packed)


def row_picks(place_ref):
    owners, docs = place_ref.shape
    tile = 2 * QUARTER
    within = iota((tile, 1), 0)
    first = within < QUARTER
    rank = (within % QUARTER).astype(F32)
    places = [
        jnp.where(first, place_ref[o : o + 1], place_ref[o + 1 : o + 2]) for o in range(0, owners, 2)
    ]
    picks = []
    for start in (0, PAIRS // 2):
        picks.append(
            jnp.concatenate(
                [
                    jnp.where(p == rank + float(start + offset), 1.0, 0.0)
                    for offset in range(0, PAIRS // 2, QUARTER)
                    for p in places
                ],
                axis=0,
            ).astype(BF16)
        )
    return picks


def read_rows(ref):
    owners, _, lanes = ref.shape
    return [
        [
            jnp.concatenate(
                [ref[o + i, :, at : at + 128].astype(F32) for i in range(2)], axis=0
            )
            for o in range(0, owners, 2)
        ]
        for at in range(0, lanes, 128)
    ]


def write_rows(ref, group, pair, tile):
    at = group * 128
    ref[2 * pair, :, at : at + 128] = tile[:QUARTER].astype(BF16)
    ref[2 * pair + 1, :, at : at + 128] = tile[QUARTER:].astype(BF16)


def swap(tile):
    keep = (iota(tile.shape, 0) < QUARTER) == (iota(tile.shape, 1) < 64)
    return jnp.where(keep, tile, pltpu.roll(pltpu.roll(tile, QUARTER, 0), 64, 1))


def hidden_kernel(parts_ref, place_ref, pre_ref, sent_ref):
    pre = parts_ref[0].astype(F32)
    for shard in range(1, parts_ref.shape[0]):
        pre += parts_ref[shard].astype(F32)
    pre_ref[...] = pre
    hidden = jax.nn.silu(pre).astype(BF16)
    none = jnp.zeros_like(hidden)
    low, high = row_picks(place_ref)
    rows = lax.dot_general(
        low, jnp.concatenate([hidden, none], axis=0), NT, preferred_element_type=F32
    ) + lax.dot_general(
        high, jnp.concatenate([none, hidden], axis=0), NT, preferred_element_type=F32
    )
    pairs = sent_ref.shape[0] // 2
    for index in range(rows.shape[0] // 8):
        write_rows(sent_ref, index // pairs, index % pairs, rows[index * 8 : (index + 1) * 8])


def label_kernel(got_ref, weight_ref, pos_ref, neg_ref, back_ref, rows_ref, grad_ref):
    groups = [jnp.concatenate([swap(t) for t in tiles], axis=1) for tiles in read_rows(got_ref)]
    groups.append(jnp.zeros_like(groups[0]))
    rows = jnp.concatenate(groups, axis=0).astype(BF16)
    rows_ref[...] = rows
    weight = weight_ref[...]
    logit = lax.dot_general(rows, weight, NT, preferred_element_type=F32)
    sig = jax.nn.sigmoid(logit)
    grad_pos = (sig - 1.0).astype(BF16).astype(F32)
    grad_neg = sig.astype(BF16).astype(F32)
    grad = (pos_ref[...] * grad_pos + neg_ref[...] * grad_neg).astype(BF16)
    grad_ref[...] = grad
    terms = jnp.dot(grad, weight, preferred_element_type=F32)
    for group in range(PAIRS // 8):
        for pair in range(back_ref.shape[0] // 2):
            tile = terms[group * 8 : (group + 1) * 8, pair * 128 : (pair + 1) * 128]
            write_rows(back_ref, group, pair, swap(tile))


def collect_kernel(came_ref, place_ref, out_ref):
    came = jnp.concatenate([t for tiles in read_rows(came_ref) for t in tiles], axis=0).astype(BF16)
    cols = out_ref.shape[1]
    low, high = row_picks(place_ref)
    tn = (((0,), (0,)), ((), ()))
    part = (
        lax.dot_general(came, low, tn, preferred_element_type=F32)[:cols]
        + lax.dot_general(came, high, tn, preferred_element_type=F32)[cols:]
    ).astype(BF16)
    for shard in range(out_ref.shape[0]):
        out_ref[shard] = part


def local_call(kernel, inputs, *shapes):
    return pl.pallas_call(
        kernel,
        out_shape=tuple(jax.ShapeDtypeStruct(shape, kind) for shape, kind in shapes),
        in_specs=[VMEM] * len(inputs),
        out_specs=(VMEM,) * len(shapes),
        compiler_params=pltpu.CompilerParams(vmem_limit_bytes=16 << 20),
    )(*inputs)


def on_device(doc_blocks, doc_counts, doc_values, pos_labels, neg_labels, in_weight, out_weight):
    block_count, block_size, col_count = in_weight.shape
    doc_total, slot_count = doc_blocks.shape
    lab_count, hidden_width = out_weight.shape
    owners = lax.axis_size("label")
    shards = lax.axis_size("feat")
    groups = doc_total // GROUP
    packed, first, chunks, copies, base, pairs, pos_count, neg_count = forward(
        doc_blocks.T,
        doc_counts,
        pos_labels.T,
        neg_labels.T,
        doc_values.reshape(groups, GROUP * slot_count, block_size),
        jnp.swapaxes(in_weight, 1, 2),
        shards,
        owners,
        lab_count,
    )
    place = jnp.where(pairs > 0, base, -1.0)
    arrived = lax.all_to_all(copies, "feat", 0, 0, tiled=True)
    row_shape = (owners, QUARTER, PAIRS * col_count // QUARTER)
    pre_t, sent = local_call(
        hidden_kernel, (arrived, place), (copies.shape[1:], F32), (row_shape, BF16)
    )
    got = lax.all_to_all(sent, "label", 0, 0, tiled=True)
    back, rows, label_grad = local_call(
        label_kernel,
        (got, out_weight, pos_count, neg_count),
        (row_shape, BF16),
        ((PAIRS + 8, hidden_width), BF16),
        ((PAIRS + 8, lab_count), BF16),
    )
    came = lax.all_to_all(back, "label", 0, 0, tiled=True)
    (copies,) = local_call(collect_kernel, (came, place), (copies.shape, BF16))
    out_grad = lax.dot_general(
        label_grad, rows, (((0,), (0,)), ((), ())), preferred_element_type=F32
    ).astype(BF16)
    copies, out_grad = lax.optimization_barrier((copies, out_grad))
    parts = lax.all_to_all(copies, "feat", 0, 0, tiled=True)
    in_grad = backward(chunks, parts, pre_t, first, packed, block_count)
    return (jnp.swapaxes(in_grad, 1, 2), out_grad)


def solution(mesh):
    placed = (P(), P(), P(), P(), P(), P("feat", None, "label"), P(("feat", "label"), None))
    return jax.shard_map(
        on_device,
        mesh=mesh,
        in_specs=placed,
        out_specs=(P("feat", None, "label"), P(("feat", "label"), None)),
        check_vma=False,
    )
```
